32 devices in a mesh: groups: 2 (over y), leaf: 4 (over z), chan: 4 (over x, core).
Axes of the slice: x: 2, y: 2, z: 4, core: 2. Of those that a mesh axis runs over, the one named last changes fastest.
Arguments:
- currents: bfloat16 [64, 32, 256], P(('groups', 'chan'), 'leaf'), parts along dimension 0, may hold values from -6 to 6
- counts: int32 [64], P(('groups', 'leaf')), parts along dimension 0, may hold values from 64 to 256
- near_list: int32 [64, 6], P(('groups', 'leaf')), parts along dimension 0, may hold values from 0 to 31, as said below
- m2l_list: int32 [8, 16], P(('groups', 'leaf')), parts along dimension 0, may hold values from 0 to 3
- m2l_type: int32 [8, 16], P(('groups', 'leaf')), parts along dimension 0, may hold values from 0 to 63
- interp: bfloat16 [64, 256, 216], P(('groups', 'leaf')), parts along dimension 0, may hold values from -0.375 to 0.375
- compress: bfloat16 [4, 216, 64], replicated, may hold values from -0.4375 to 0.4375
- m2m: bfloat16 [4, 8, 64, 64], replicated, may hold values from -0.25 to 0.25
- m2l: bfloat16 [4, 64, 64, 64], replicated, may hold values from -0.1875 to 0.1875
- near_tiles: bfloat16 [64, 6, 256, 256], P(('groups', 'leaf')), parts along dimension 0, may hold values from -0.15625 to 0.15625
- jacobi: bfloat16 [64, 256, 256], P(('groups', 'leaf')), parts along dimension 0
Outputs:
- applied: float32 [64, 32, 256], P(('groups', 'chan'), 'leaf'), parts along dimension 0
The draws below stay inside these ranges and needn't reach their ends.
There are 2 independent parts, one for each index of `groups`. The reference program is written for one: setup_inputs(seed, part) draws one part's arguments, and reference() takes and returns one part's arrays. A program takes and returns all parts, laid end to end along the dimension named above; an argument that names none is the same for every part. Nothing has to cross between parts.
Inputs may be any that keep to these rules, and one draw needn't show every extreme that they name: near_list[l, 0] = l, and every entry lies within 8 leaves of l.
All inputs are finite; a program needn't handle non-finite values.
Results may differ from the reference program's by a relative error of at most 0.0035.
Values may be sent and summed in bfloat16 or wider, within the bound.
No kernel may reach another device: no remote copies, remote signals or barrier semaphores. Data moves between devices by JAX's collectives and lax.ppermute only.
A program may use at most 64 MiB of HBM per device.

```python
import jax
import jax.numpy as jnp

C = 4
INC = 8
UNK = 256
NODES = 216
RANK = 64
NTYPES = 64
NLIST = 16
NNB = 6
LEAVES_DEV = 8
LEAVES = 32
PARENTS = 4
COMBOS = 32


def draw_counts(key, part):
    key = jax.random.fold_in(key, 11)
    values = jax.random.randint(key, (LEAVES,), UNK // 4, UNK + 1)
    values = values.at[0].set(UNK).at[1].set(UNK // 4)
    return values.astype(jnp.int32)


def draw_near_list(key, part):
    key = jax.random.fold_in(key, 12)
    offsets = jax.random.randint(key, (LEAVES, NNB), -LEAVES_DEV, LEAVES_DEV + 1)
    offsets = offsets.at[:, 0].set(0)
    ids = jnp.arange(LEAVES, dtype=jnp.int32)[:, None] + offsets
    return jnp.clip(ids, 0, LEAVES - 1).astype(jnp.int32)


def draw_jacobi(key, part):
    key = jax.random.fold_in(key, 13)
    noise = jax.random.normal(key, (LEAVES, UNK, UNK), jnp.float32)
    eye = jnp.eye(UNK, dtype=jnp.float32)
    return (eye[None] + noise * (0.5 / UNK ** 0.5)).astype(jnp.bfloat16)


def plant(drawn, stream_key, low, high):
    longest = drawn.shape.index(max(drawn.shape))
    spots = []
    for shift in (0, 1):
        where = [jax.random.randint(jax.random.fold_in(stream_key, axis), (), 0, length) for axis, length in enumerate(drawn.shape)]
        where[longest] = (where[longest] + shift) % drawn.shape[longest]
        spots.append(tuple(where))
    return drawn.at[spots[0]].set(low).at[spots[1]].set(high)


def level_of(stream_key, shape, shards, least, largest):
    factor_of, own = 1.0, jax.random.fold_in(stream_key, 6)
    for position, shards_of in shards:
        draws = jnp.exp(jax.random.uniform(jax.random.fold_in(own, position), (shards_of,), jnp.float32, least / len(shards), largest / len(shards)))
        factor_of = factor_of * jnp.repeat(draws, shape[position] // shards_of).reshape([-1 if axis == position else 1 for axis in range(len(shape))])
    return factor_of


def gaussian(stream_key, shape, deviation, most, split=(), kind=jnp.bfloat16):
    array = deviation * jax.random.normal(stream_key, shape, jnp.float32)
    if split:
        array = array * level_of(stream_key, shape, split, -0.22, 0.18)
    return jnp.clip(array, -most, most).astype(kind)


def setup_inputs(seed: int = 0, part: int = 0) -> dict:
    seeds = jax.random.split(jax.random.key(seed), 12)
    part_keys = jax.random.split(jax.random.fold_in(seeds[11], part), 12)
    return {
        "currents": gaussian(part_keys[0], (COMBOS, LEAVES, UNK), 1.0, 6.0, ((0, 4), (1, 4))),
        "counts": draw_counts(jax.random.fold_in(jax.random.fold_in(seeds[11], part), 71), part),
        "near_list": draw_near_list(jax.random.fold_in(jax.random.fold_in(seeds[11], part), 71), part),
        "m2l_list": plant(jax.random.randint(part_keys[3], (PARENTS, NLIST), 0, PARENTS), jax.random.fold_in(part_keys[3], 1), 0, PARENTS - 1).astype(jnp.int32),
        "m2l_type": plant(jax.random.randint(part_keys[4], (PARENTS, NLIST), 0, NTYPES), jax.random.fold_in(part_keys[4], 1), 0, NTYPES - 1).astype(jnp.int32),
        "interp": gaussian(part_keys[5], (LEAVES, UNK, NODES), UNK ** -0.5, 0.375, ((0, 4),)),
        "compress": gaussian(seeds[6], (C, NODES, RANK), NODES ** -0.5, 0.4375),
        "m2m": gaussian(seeds[7], (C, 8, RANK, RANK), (8 * RANK) ** -0.5, 0.25),
        "m2l": gaussian(seeds[8], (C, NTYPES, RANK, RANK), (NLIST * RANK) ** -0.5, 0.1875),
        "near_tiles": gaussian(part_keys[9], (LEAVES, NNB, UNK, UNK), (NNB * UNK) ** -0.5, 0.15625, ((0, 4),)),
        "jacobi": draw_jacobi(jax.random.fold_in(jax.random.fold_in(seeds[11], part), 71), part),
    }


def reference(currents, counts, near_list, m2l_list, m2l_type, interp, compress, m2m, m2l, near_tiles, jacobi):
    slots = jnp.arange(UNK, dtype=jnp.int32)
    live = slots[None, :] < counts[:, None]
    masked = jnp.where(live[None], currents, jnp.zeros_like(currents)).astype(jnp.bfloat16)
    gathered = masked[:, near_list].astype(jnp.float32)
    near = jnp.einsum('lkvu,qlku->qlv', near_tiles.astype(jnp.float32), gathered)
    interp_f = interp.astype(jnp.float32)
    parts = []
    for chan_id in range(C):
        block = masked[chan_id * INC:(chan_id + 1) * INC].astype(jnp.float32)
        comp = compress[chan_id].astype(jnp.float32)
        trans = m2m[chan_id].astype(jnp.float32)
        nodes = jnp.einsum('qlu,lun->qln', block, interp_f).astype(jnp.bfloat16)
        moments = jnp.einsum('qln,nr->qlr', nodes.astype(jnp.float32), comp).astype(jnp.bfloat16)
        grouped = moments.astype(jnp.float32).reshape(INC, PARENTS, 8, RANK)
        boxes = jnp.einsum('qpsr,srt->qpt', grouped, trans).astype(jnp.bfloat16)
        sources = boxes.astype(jnp.float32)[:, m2l_list]
        mats = m2l[chan_id].astype(jnp.float32)[m2l_type]
        local = jnp.einsum('qpkr,pkrt->qpt', sources, mats).astype(jnp.bfloat16)
        leaf_local = jnp.einsum('qpt,srt->qpsr', local.astype(jnp.float32), trans)
        leaf_local = leaf_local.reshape(INC, LEAVES, RANK).astype(jnp.bfloat16)
        far_nodes = jnp.einsum('qlr,nr->qln', leaf_local.astype(jnp.float32), comp).astype(jnp.bfloat16)
        far = jnp.einsum('qln,lun->qlu', far_nodes.astype(jnp.float32), interp_f)
        parts.append(far)
    far_all = jnp.concatenate(parts, axis=0)
    total = (near + far_all).astype(jnp.bfloat16)
    applied = jnp.einsum('lvu,qlu->qlv', jacobi.astype(jnp.float32), total.astype(jnp.float32))
    return jnp.where(live[None], applied, jnp.zeros_like(applied))
```

```python
import jax
import jax.numpy as jnp
from jax import lax
from jax.experimental import pallas as pl
from jax.experimental.pallas import tpu as pltpu
from jax.sharding import PartitionSpec as P

F32 = jnp.float32
BF16 = jnp.bfloat16
NT = (((1,), (1,)), ((), ()))
VMEM = pl.BlockSpec(memory_space=pltpu.VMEM)
SMEM = pl.BlockSpec(memory_space=pltpu.SMEM)
HBM = pl.BlockSpec(memory_space=pltpu.HBM)
COST = 2 * 10**9


def call(kernel, out_shape, in_specs, scratch=()):
    return pl.pallas_call(
        kernel,
        out_shape=out_shape,
        in_specs=in_specs,
        out_specs=jax.tree.map(lambda _: VMEM, out_shape),
        scratch_shapes=list(scratch),
        compiler_params=pltpu.CompilerParams(vmem_limit_bytes=16 << 20),
        cost_estimate=pl.CostEstimate(flops=COST, bytes_accessed=0, transcendentals=0),
    )


def in_hbm(*arrays):
    return [pltpu.with_memory_space_constraint(array, pltpu.HBM) for array in arrays]


def core_index():
    return lax.rem(lax.axis_index("chan"), 2)


def nt(a, b):
    return lax.dot_general(a, b, NT, preferred_element_type=F32)


def nn(a, b):
    return jnp.dot(a, b, preferred_element_type=F32)


def load_kernel(
    counts, own, interp_t, comp_t, m2m, interp_out, comp_out, m2m_out, mine, live, counts_s, own_s, sems
):
    base = lax.div(lax.axis_index("chan"), 2) * 2
    copies = [
        pltpu.make_async_copy(counts, counts_s, sems.at[0]),
        pltpu.make_async_copy(own, own_s, sems.at[1]),
        pltpu.make_async_copy(interp_t, interp_out, sems.at[2]),
        pltpu.make_async_copy(comp_t.at[pl.ds(base, 2)], comp_out, sems.at[3]),
        pltpu.make_async_copy(m2m.at[pl.ds(base, 2)], m2m_out, sems.at[4]),
    ]
    for copy in copies:
        copy.start()
    leaves, unknowns = live.shape
    slots = lax.broadcasted_iota(jnp.int32, (1, unknowns), 1)
    copies[0].wait()
    for leaf in range(leaves):
        live[leaf : leaf + 1] = jnp.where(slots < counts_s[leaf], 1.0, 0.0)
    copies[1].wait()
    mine[...] = jnp.swapaxes(own_s[...].astype(F32), 0, 1) * live[...][:, None, :]
    for copy in copies[2:]:
        copy.wait()


def box_kernel(mine, live, recv, interp_t, comp_t, m2m, packed, boxes):
    leaves, combos, unknowns = mine.shape
    rows = 2 * combos
    rank = m2m.shape[2]
    core = core_index()
    own = mine[...]
    other = jnp.swapaxes(recv[...].astype(F32), 0, 1) * live[...][:, None, :]
    both = jnp.concatenate([jnp.where(core == 1, other, own), own], axis=1).astype(BF16)
    packed[0:leaves] = both

    @pl.when(core == 0)
    def _():
        packed[leaves] = jnp.zeros((rows, unknowns), BF16)
        boxes[...] = jnp.zeros_like(boxes)

    @pl.when(core == 1)
    def _():
        nodes = jnp.concatenate(
            [nt(both[leaf], interp_t[leaf]).astype(BF16) for leaf in range(leaves)], axis=0
        )
        comp = comp_t[...].reshape(2 * rank, comp_t.shape[2])
        moments = nt(nodes, comp)
        row = lax.broadcasted_iota(jnp.int32, moments.shape, 0)
        lane = lax.broadcasted_iota(jnp.int32, moments.shape, 1)
        same = (lax.rem(row, rows) >= combos) == (lane >= rank)
        moments = jnp.where(same, moments, 0.0).astype(BF16)
        total = None
        for leaf in range(leaves):
            trans = jnp.concatenate([m2m[0, leaf], m2m[1, leaf]], axis=0)
            part = nn(moments[leaf * rows : (leaf + 1) * rows], trans)
            total = part if total is None else total + part
        wide = jnp.concatenate([total, jnp.zeros((rows, unknowns - rank), F32)], axis=1).astype(BF16)
        packed[leaves] = wide
        boxes[0] = wide


def local_kernel(near_list, m2l_type, mine, tiles, table, near, mats, own, sems):
    chan = lax.axis_index("chan")
    me = lax.axis_index("leaf")
    entries = mats.shape[0]
    leaves, neighbours = near_list.shape
    copies = [
        pltpu.make_async_copy(table.at[chan, m2l_type[0, k]], mats.at[k], sems.at[k])
        for k in range(entries)
    ]
    for copy in copies:
        copy.start()
    own[0:leaves] = mine[...]
    own[leaves] = jnp.zeros(own.shape[1:], F32)
    for leaf in range(leaves):
        total = None
        for k in range(neighbours):
            place = near_list[leaf, k] - me * leaves
            place = jnp.where(jnp.logical_and(place >= 0, place < leaves), place, leaves)
            part = nt(own[place].astype(BF16), tiles[leaf, k])
            total = part if total is None else total + part
        near[leaf] = total
    for copy in copies:
        copy.wait()


def final_kernel(
    near_list, m2l_list, live, here, swapped, boxes_own, mats, near, tiles, interp_t, comp_t, m2m, jacobi,
    out, beside, sources,
):
    core = core_index()
    me = lax.axis_index("leaf")
    count = sources.shape[0]
    entries = mats.shape[0]
    leaves, neighbours = near_list.shape
    combos, unknowns = near.shape[1:]
    rank = mats.shape[1]
    first = core == 0
    wide = leaves + 1

    def mine(block):
        block = block.astype(F32)
        return jnp.where(first, block[..., :combos, :], block[..., combos:, :])

    def received(start, size):
        return mine(jnp.where(first, here[start : start + size], swapped[start : start + size]))

    odd = lax.rem(me, 2) == 1
    box_a, box_b = received(leaves, 1)[0], received(wide + leaves, 1)[0]
    sources[0] = mine(jnp.where(first, swapped[2 * wide + count - 3], boxes_own[0]))
    sources[1] = jnp.where(odd, box_a, box_b)
    sources[count - 1] = jnp.where(odd, box_b, box_a)
    for s in range(2, count - 1):
        sources[s] = received(2 * wide + s - 2, 1)[0]

    low = received(0, leaves)
    high = received(wide, leaves)
    beside[0:leaves] = jnp.where(odd, low, high)
    beside[leaves : 2 * leaves] = jnp.where(odd, high, low)
    beside[2 * leaves] = jnp.zeros((combos, unknowns), F32)

    local = None
    for k in range(entries):
        step = lax.rem(me - m2l_list[0, k] + count, count)
        part = nn(sources[step][:, :rank].astype(BF16), mats[k])
        local = part if local is None else local + part
    local = local.astype(BF16)

    def near_of(leaf):
        total = near[leaf]
        for k in range(neighbours):
            place = near_list[leaf, k] - me * leaves
            place = jnp.where(
                place < 0, place + leaves, jnp.where(place >= leaves, place, 2 * leaves)
            )
            total = total + nt(beside[place].astype(BF16), tiles[leaf, k])
        return total

    half = leaves // 2
    sums = [near_of(leaf) for leaf in range(half)]
    leaf_local = jnp.concatenate(
        [nt(local, m2m[core, leaf]).astype(BF16) for leaf in range(leaves)], axis=0
    )
    sums += [near_of(leaf) for leaf in range(half, leaves)]
    far_nodes = nn(leaf_local, comp_t[core]).astype(BF16)
    for leaf in range(leaves):
        far = nn(far_nodes[leaf * combos : (leaf + 1) * combos], interp_t[leaf])
        applied = nt((sums[leaf] + far).astype(BF16), jacobi[leaf])
        out[:, leaf, :] = applied * live[leaf : leaf + 1]


def body(
    currents, counts, near_list, m2l_list, m2l_type, interp, compress, m2m, m2l, near_tiles, jacobi
):
    combos, leaves, unknowns = currents.shape
    nodes, rank = compress.shape[1:]
    entries = m2l_list.shape[1]
    n = lax.axis_size("leaf")
    chans = lax.axis_size("chan")
    axes = ("leaf", "chan")
    shape = jax.ShapeDtypeStruct

    def permute(value, target):
        moves = []
        for leaf in range(n):
            for c in range(0, chans, 2):
                for core in (0, 1):
                    to_leaf, to_core = target(leaf, core)
                    moves.append((leaf * chans + c + core, (to_leaf % n) * chans + c + to_core))
        return lax.ppermute(value, axes, moves)

    def swap(value):
        return permute(value, lambda leaf, core: (leaf, 1 - core))

    def gather(value, to_leaf):
        return permute(value, lambda leaf, core: (to_leaf(leaf), 0) if core else (leaf, 1))

    recv = swap(currents)
    interp_v, comp_v, m2m_v, mine, live = call(
        load_kernel,
        (
            shape((leaves, nodes, unknowns), BF16),
            shape((2, rank, nodes), BF16),
            shape((2, leaves, rank, rank), BF16),
            shape((leaves, combos, unknowns), F32),
            shape((leaves, unknowns), F32),
        ),
        [HBM] * 5,
        [
            pltpu.SMEM((leaves,), jnp.int32),
            pltpu.VMEM(currents.shape, BF16),
            pltpu.SemaphoreType.DMA((5,)),
        ],
    )(*in_hbm(counts, currents, jnp.swapaxes(interp, 1, 2), jnp.swapaxes(compress, 1, 2), m2m))
    packed, boxes = call(
        box_kernel,
        (
            shape((leaves + 1, 2 * combos, unknowns), BF16),
            shape((1, 2 * combos, unknowns), BF16),
        ),
        [VMEM] * 6,
    )(mine, live, recv, interp_v, comp_v, m2m_v)
    even_a = gather(packed, lambda leaf: leaf ^ 1)
    even_b = gather(packed, lambda leaf: leaf + 1 if leaf % 2 else leaf - 1)
    rest = [gather(boxes, lambda leaf, s=s: leaf + s) for s in range(2, n - 1)]
    near, mats = call(
        local_kernel,
        (shape((leaves, combos, unknowns), F32), shape((entries, rank, rank), BF16)),
        [SMEM, SMEM, VMEM, VMEM, HBM],
        [
            pltpu.VMEM((leaves + 1, combos, unknowns), F32),
            pltpu.SemaphoreType.DMA((entries,)),
        ],
    )(near_list, m2l_type, mine, near_tiles, *in_hbm(m2l))
    here = jnp.concatenate([even_a, even_b, *rest, boxes], axis=0)
    here, near = lax.optimization_barrier((here, near))
    swapped = swap(here)
    return call(
        final_kernel,
        shape(currents.shape, F32),
        [SMEM, SMEM] + [VMEM] * 11,
        [
            pltpu.VMEM((2 * leaves + 1, combos, unknowns), F32),
            pltpu.VMEM((n, combos, unknowns), F32),
        ],
    )(
        near_list, m2l_list, live, here, swapped, boxes, mats, near, near_tiles, interp_v, comp_v, m2m_v, jacobi,
    )


def solution(mesh):
    placed = (
        P(("groups", "chan"), "leaf", None),
        P(("groups", "leaf")),
        P(("groups", "leaf"), None),
        P(("groups", "leaf"), None),
        P(("groups", "leaf"), None),
        P(("groups", "leaf"), None, None),
        P(),
        P(),
        P(),
        P(("groups", "leaf"), None, None, None),
        P(("groups", "leaf"), None, None),
    )
    return jax.shard_map(
        body,
        mesh=mesh,
        in_specs=placed,
        out_specs=P(("groups", "chan"), "leaf", None),
        check_vma=False,
    )
```

```python
import jax
import jax.numpy as jnp
from jax import lax
from jax.experimental import pallas as pl
from jax.experimental.pallas import tpu as pltpu
from jax.sharding import PartitionSpec as P

F32 = jnp.float32
BF16 = jnp.bfloat16
NT = (((1,), (1,)), ((), ()))
VMEM = pl.BlockSpec(memory_space=pltpu.VMEM)
SMEM = pl.BlockSpec(memory_space=pltpu.SMEM)
HBM = pl.BlockSpec(memory_space=pltpu.HBM)
COST = 2 * 10**9


def call(kernel, out_shape, in_specs, scratch=()):
    return pl.pallas_call(
        kernel,
        out_shape=out_shape,
        in_specs=in_specs,
        out_specs=jax.tree.map(lambda _: VMEM, out_shape),
        scratch_shapes=list(scratch),
        compiler_params=pltpu.CompilerParams(vmem_limit_bytes=16 << 20),
        cost_estimate=pl.CostEstimate(flops=COST, bytes_accessed=0, transcendentals=0),
    )


def in_hbm(*arrays):
    return [pltpu.with_memory_space_constraint(array, pltpu.HBM) for array in arrays]


def core_index():
    return lax.rem(lax.axis_index("chan"), 2)


def nt(a, b):
    return lax.dot_general(a, b, NT, preferred_element_type=F32)


def nn(a, b):
    return jnp.dot(a, b, preferred_element_type=F32)


def halves(value):
    high = value.astype(BF16)
    return jnp.concatenate([high, (value - high.astype(F32)).astype(BF16)], axis=0)


def halves_sum(value):
    half = value.shape[0] // 2
    return value[:half] + value[half:]


def load_kernel(
    counts, own, interp_t, comp_t, m2m, interp_out, comp_out, m2m_out, mine, live, counts_s, own_s, sems
):
    base = lax.div(lax.axis_index("chan"), 2) * 2
    far = core_index() == 1
    first = [
        pltpu.make_async_copy(counts, counts_s, sems.at[0]),
        pltpu.make_async_copy(own, own_s, sems.at[1]),
    ]
    tables = [
        pltpu.make_async_copy(interp_t, interp_out, sems.at[2]),
        pltpu.make_async_copy(comp_t.at[pl.ds(base, 2)], comp_out, sems.at[3]),
        pltpu.make_async_copy(m2m.at[pl.ds(base, 2)], m2m_out, sems.at[4]),
    ]
    for copy in first:
        copy.start()

    @pl.when(far)
    def _():
        for copy in tables:
            copy.start()

    leaves, unknowns = live.shape
    slots = lax.broadcasted_iota(jnp.int32, (1, unknowns), 1)
    first[0].wait()
    for leaf in range(leaves):
        live[leaf : leaf + 1] = jnp.where(slots < counts_s[leaf], 1.0, 0.0)
    first[1].wait()
    mine[...] = jnp.swapaxes(own_s[...].astype(F32), 0, 1) * live[...][:, None, :]

    @pl.when(far)
    def _():
        for copy in tables:
            copy.wait()


def by_channel(rows, combos, rank):
    row = lax.broadcasted_iota(jnp.int32, (rows, 2 * rank), 0)
    lane = lax.broadcasted_iota(jnp.int32, (rows, 2 * rank), 1)
    return (lax.rem(row, 2 * combos) >= combos) == (lane >= rank)


def box_kernel(mine, live, recv, interp_t, comp_t, m2m, packed, boxes):
    leaves, combos, unknowns = mine.shape
    rows = 2 * combos
    rank = m2m.shape[2]
    core = core_index()
    own = mine[...]
    other = jnp.swapaxes(recv[...].astype(F32), 0, 1) * live[...][:, None, :]
    both = jnp.concatenate(
        [jnp.where(core == 1, other, own), jnp.where(core == 1, own, other)], axis=1
    ).astype(BF16)
    packed[0:leaves] = both

    @pl.when(core == 0)
    def _():
        packed[leaves] = jnp.zeros((rows, unknowns), BF16)
        boxes[...] = jnp.zeros_like(boxes)

    @pl.when(core == 1)
    def _():
        nodes = jnp.concatenate(
            [nt(both[leaf], interp_t[leaf]).astype(BF16) for leaf in range(leaves)], axis=0
        )
        comp = comp_t[...].reshape(2 * rank, comp_t.shape[2])
        moments = nt(nodes, comp)
        moments = jnp.where(by_channel(leaves * rows, combos, rank), moments, 0.0).astype(BF16)
        total = None
        for leaf in range(leaves):
            trans = jnp.concatenate([m2m[0, leaf], m2m[1, leaf]], axis=0)
            part = nn(moments[leaf * rows : (leaf + 1) * rows], trans)
            total = part if total is None else total + part
        pair = jnp.concatenate([total, total], axis=1)
        pair = jnp.where(by_channel(rows, combos, rank), pair, 0.0).astype(BF16)
        boxes[0] = pair
        packed[leaves] = jnp.concatenate(
            [pair, jnp.zeros((rows, unknowns - 2 * rank), BF16)], axis=1
        )


def near_kernel(near_list, packed, by_pair, by_edge, tiles, jacobi, near, beside):
    me = lax.axis_index("leaf")
    leaves, neighbours = near_list.shape

    @pl.when(core_index() == 0)
    def _():
        odd = lax.rem(me, 2) == 1
        pair = by_pair[0:leaves].astype(F32)
        edge = by_edge[0:leaves].astype(F32)
        beside[0:leaves] = jnp.where(odd, pair, edge)
        beside[leaves : 2 * leaves] = packed[0:leaves].astype(F32)
        beside[2 * leaves : 3 * leaves] = jnp.where(odd, edge, pair)
        start = (me - 1) * leaves
        sums = []
        for leaf in range(leaves):
            total = None
            for k in range(neighbours):
                part = nt(beside[near_list[leaf, k] - start].astype(BF16), tiles[leaf, k])
                total = part if total is None else total + part
            sums.append(halves(total))
        for leaf in range(leaves):
            near[leaf] = halves_sum(nt(sums[leaf], jacobi[leaf]))


def expand_kernel(interp_t, comp_t, out):
    @pl.when(core_index() == 1)
    def _():
        comp = comp_t[...].reshape(-1, comp_t.shape[2])
        for leaf in range(out.shape[0]):
            out[leaf] = halves(nn(comp, interp_t[leaf]))


def apply_kernel(expand, jacobi, out):
    @pl.when(core_index() == 1)
    def _():
        for leaf in range(out.shape[0]):
            out[leaf] = halves(halves_sum(nt(expand[leaf], jacobi[leaf])))


def source_kernel(m2l_list, m2l_type, table, out, sums):
    me = lax.axis_index("leaf")
    base = lax.div(lax.axis_index("chan"), 2) * 2
    rank = table.shape[2]

    @pl.when(core_index() == 1)
    def _():
        sums[...] = jnp.zeros_like(sums)
        for k in range(m2l_list.shape[1]):
            slot = jnp.bitwise_xor(m2l_list[0, k], me)
            kind = m2l_type[0, k]
            sums[slot, :rank] += table[base, kind].astype(F32)
            sums[slot, rank:] += table[base + 1, kind].astype(F32)
        for slot in range(out.shape[0]):
            out[slot] = halves(sums[slot])


def far_kernel(boxes, sources, near, m2m, apply, keep, send):
    core = core_index()
    leaves, rows = near.shape[:2]
    combos = rows // 2
    rank = m2m.shape[2]

    @pl.when(core == 0)
    def _():
        keep[...] = near[:, :combos]
        send[...] = near[:, combos:]

    @pl.when(core == 1)
    def _():
        local = None
        for slot in range(boxes.shape[0]):
            box = boxes[slot]
            part = nn(jnp.concatenate([box, box], axis=1), sources[slot])
            local = part if local is None else local + part
        local = local.astype(BF16)
        mask = by_channel(rows, combos, rank)
        down = []
        for leaf in range(leaves):
            trans = jnp.concatenate([m2m[0, leaf], m2m[1, leaf]], axis=0)
            down.append(jnp.where(mask, nt(local, trans), 0.0).astype(BF16))
        for leaf in range(leaves):
            far = nn(jnp.concatenate([down[leaf], down[leaf]], axis=1), apply[leaf])
            keep[leaf] = far[combos:]
            send[leaf] = far[:combos]


def final_kernel(live, keep, recv, out):
    total = (keep[...] + recv[...]) * live[...][:, None, :]
    out[...] = jnp.swapaxes(total, 0, 1)


def body(
    currents, counts, near_list, m2l_list, m2l_type, interp, compress, m2m, m2l, near_tiles, jacobi
):
    combos, leaves, unknowns = currents.shape
    nodes, rank = compress.shape[1:]
    rows = 2 * combos
    entries = m2l_list.shape[1]
    n = lax.axis_size("leaf")
    chans = lax.axis_size("chan")
    shape = jax.ShapeDtypeStruct

    def permute(value, target):
        moves = []
        for leaf in range(n):
            for chan in range(chans):
                to_leaf, to_chan = target(leaf, chan)
                moves.append((leaf * chans + chan, to_leaf * chans + to_chan))
        return lax.ppermute(value, ("leaf", "chan"), moves)

    def swap(value):
        return permute(value, lambda leaf, chan: (leaf, chan ^ 1))

    def edge(leaf, chan):
        if leaf in (0, n - 1) or chan % 2:
            return leaf, chan ^ 2
        return (leaf + 1 if leaf % 2 else leaf - 1), chan

    recv = swap(currents)
    interp_v, comp_v, m2m_v, mine, live = call(
        load_kernel,
        (
            shape((leaves, nodes, unknowns), BF16),
            shape((2, rank, nodes), BF16),
            shape((2, leaves, rank, rank), BF16),
            shape((leaves, combos, unknowns), F32),
            shape((leaves, unknowns), F32),
        ),
        [HBM] * 5,
        [
            pltpu.SMEM((leaves,), jnp.int32),
            pltpu.VMEM(currents.shape, BF16),
            pltpu.SemaphoreType.DMA((5,)),
        ],
    )(*in_hbm(counts, currents, jnp.swapaxes(interp, 1, 2), jnp.swapaxes(compress, 1, 2), m2m))
    packed, boxes = call(
        box_kernel,
        (shape((leaves + 1, rows, unknowns), BF16), shape((1, rows, 2 * rank), BF16)),
        [VMEM] * 6,
    )(mine, live, recv, interp_v, comp_v, m2m_v)
    double = shape((leaves, 4 * rank, unknowns), BF16)
    by_pair = permute(packed, lambda leaf, chan: (leaf ^ 1, chan))
    comp_v, after = lax.optimization_barrier((comp_v, packed))
    expand = call(expand_kernel, double, [VMEM] * 2)(interp_v, comp_v)
    after, expand = lax.optimization_barrier((after, expand))
    by_edge = permute(after, edge)
    m2l, expand = lax.optimization_barrier((m2l, expand))
    sources = call(
        source_kernel,
        shape((n, 4 * rank, rank), BF16),
        [SMEM, SMEM, VMEM],
        [pltpu.VMEM((n, 2 * rank, rank), F32)],
    )(m2l_list, m2l_type, m2l)
    boxes = jnp.concatenate([boxes, by_pair[leaves:, :, : 2 * rank]], axis=0)
    boxes, expand, sources = lax.optimization_barrier((boxes, expand, sources))
    apply = call(apply_kernel, double, [VMEM] * 2)(expand, jacobi)
    step = 2
    while step < n:
        boxes = jnp.concatenate(
            [
                boxes,
                permute(
                    boxes,
                    lambda leaf, chan, step=step: (leaf ^ step, chan) if chan % 2 else (leaf, chan ^ 2),
                ),
            ],
            axis=0,
        )
        step *= 2
    near = call(
        near_kernel,
        shape((leaves, rows, unknowns), F32),
        [SMEM, VMEM, VMEM, VMEM, VMEM, VMEM],
        [pltpu.VMEM((3 * leaves, rows, unknowns), F32)],
    )(near_list, packed, by_pair, by_edge, near_tiles, jacobi)
    part = shape((leaves, combos, unknowns), F32)
    keep, send = call(far_kernel, (part, part), [VMEM] * 5)(boxes, sources, near, m2m_v, apply)
    return call(final_kernel, shape(currents.shape, F32), [VMEM] * 3)(live, keep, swap(send))


def solution(mesh):
    placed = (
        P(("groups", "chan"), "leaf", None),
        P(("groups", "leaf")),
        P(("groups", "leaf"), None),
        P(("groups", "leaf"), None),
        P(("groups", "leaf"), None),
        P(("groups", "leaf"), None, None),
        P(),
        P(),
        P(),
        P(("groups", "leaf"), None, None, None),
        P(("groups", "leaf"), None, None),
    )
    return jax.shard_map(
        body,
        mesh=mesh,
        in_specs=placed,
        out_specs=P(("groups", "chan"), "leaf", None),
        check_vma=False,
    )
```

```python
import jax
import jax.numpy as jnp
from jax import lax
from jax.experimental import pallas as pl
from jax.experimental.pallas import tpu as pltpu
from jax.sharding import PartitionSpec as P

F32 = jnp.float32
BF16 = jnp.bfloat16
NT = (((1,), (1,)), ((), ()))
VMEM = pl.BlockSpec(memory_space=pltpu.VMEM)
HBM = pl.BlockSpec(memory_space=pltpu.HBM)
COST = 2 * 10**9
AHEAD = 2


def call(kernel, out_shape, in_specs, scratch=()):
    return pl.pallas_call(
        kernel,
        out_shape=out_shape,
        in_specs=in_specs,
        out_specs=jax.tree.map(lambda _: VMEM, out_shape),
        scratch_shapes=list(scratch),
        compiler_params=pltpu.CompilerParams(vmem_limit_bytes=16 << 20),
        cost_estimate=pl.CostEstimate(flops=COST, bytes_accessed=0, transcendentals=0),
    )


def in_hbm(*arrays):
    return [pltpu.with_memory_space_constraint(array, pltpu.HBM) for array in arrays]


def core_index():
    return lax.rem(lax.axis_index("chan"), 2)


def nt(a, b):
    return lax.dot_general(a, b, NT, preferred_element_type=F32)


def nn(a, b):
    return jnp.dot(a, b, preferred_element_type=F32)


def halves(value):
    high = value.astype(BF16)
    return jnp.concatenate([high, (value - high.astype(F32)).astype(BF16)], axis=0)


def halves_sum(value):
    half = value.shape[0] // 2
    return value[:half] + value[half:]


def load_kernel(counts, own, mine, live, counts_s, own_s, sems):
    copies = [
        pltpu.make_async_copy(counts, counts_s, sems.at[0]),
        pltpu.make_async_copy(own, own_s, sems.at[1]),
    ]
    for copy in copies:
        copy.start()
    leaves, unknowns = live.shape
    slots = lax.broadcasted_iota(jnp.int32, (1, unknowns), 1)
    copies[0].wait()
    for leaf in range(leaves):
        live[leaf : leaf + 1] = jnp.where(slots < counts_s[leaf], 1.0, 0.0)
    copies[1].wait()
    mine[...] = jnp.swapaxes(own_s[...].astype(F32), 0, 1) * live[...][:, None, :]


def chip_base():
    return lax.div(lax.axis_index("chan"), 2) * 2


def chip_pair(table):
    pair = table[pl.ds(chip_base(), 2)]
    return pair.reshape(-1, table.shape[2])


def chip_m2m(m2m, leaf):
    base = chip_base()
    return jnp.concatenate([m2m[base, leaf], m2m[base + 1, leaf]], axis=0)


def by_channel(rows, combos, rank):
    row = lax.broadcasted_iota(jnp.int32, (rows, 2 * rank), 0)
    lane = lax.broadcasted_iota(jnp.int32, (rows, 2 * rank), 1)
    return (lax.rem(row, 2 * combos) >= combos) == (lane >= rank)


def box_kernel(mine, live, recv, interp_t, comp_t, m2m, packed, boxes):
    leaves, combos, unknowns = mine.shape
    rows = 2 * combos
    rank = m2m.shape[2]
    core = core_index()
    own = mine[...]
    other = jnp.swapaxes(recv[...].astype(F32), 0, 1) * live[...][:, None, :]
    both = jnp.concatenate(
        [jnp.where(core == 1, other, own), jnp.where(core == 1, own, other)], axis=1
    ).astype(BF16)
    packed[0:leaves] = both

    @pl.when(core == 0)
    def _():
        packed[leaves] = jnp.zeros((rows, unknowns), BF16)
        boxes[...] = jnp.zeros_like(boxes)

    @pl.when(core == 1)
    def _():
        nodes = jnp.concatenate(
            [nt(both[leaf], interp_t[leaf]).astype(BF16) for leaf in range(leaves)], axis=0
        )
        comp = chip_pair(comp_t)
        moments = nt(nodes, comp)
        moments = jnp.where(by_channel(leaves * rows, combos, rank), moments, 0.0).astype(BF16)
        total = None
        for leaf in range(leaves):
            trans = chip_m2m(m2m, leaf)
            part = nn(moments[leaf * rows : (leaf + 1) * rows], trans)
            total = part if total is None else total + part
        pair = jnp.concatenate([total, total], axis=1)
        pair = jnp.where(by_channel(rows, combos, rank), pair, 0.0).astype(BF16)
        boxes[0] = pair
        packed[leaves] = jnp.concatenate(
            [pair, jnp.zeros((rows, unknowns - 2 * rank), BF16)], axis=1
        )


def near_kernel(near_list, packed, by_pair, by_edge, tiles, turned, first, jacobi, near, beside):
    me = lax.axis_index("leaf")
    leaves, neighbours = near_list.shape
    ahead = turned.shape[1]

    @pl.when(core_index() == 0)
    def _():
        places = near_list[...] - (me - 1) * leaves
        odd = lax.rem(me, 2) == 1
        pair = by_pair[0:leaves].astype(F32)
        edge = by_edge[0:leaves].astype(F32)
        beside[0:leaves] = jnp.where(odd, pair, edge)
        beside[leaves : 2 * leaves] = packed[0:leaves].astype(F32)
        beside[2 * leaves : 3 * leaves] = jnp.where(odd, edge, pair)
        sums = []
        for leaf in range(leaves):
            total = first[leaf]
            for k in range(1, neighbours):
                x = beside[places[leaf, k]].astype(BF16)
                if k <= ahead:
                    total = total + nn(x, turned[leaf, k - 1])
                else:
                    total = total + nt(x, tiles[leaf, k])
            sums.append(halves(total))
        for leaf in range(leaves):
            near[leaf] = halves_sum(nt(sums[leaf], jacobi[leaf]))


def expand_kernel(interp_t, comp_t, out):
    @pl.when(core_index() == 1)
    def _():
        comp = chip_pair(comp_t)
        for leaf in range(out.shape[0]):
            out[leaf] = halves(nn(comp, interp_t[leaf]))


def apply_kernel(expand, jacobi, out):
    @pl.when(core_index() == 1)
    def _():
        for leaf in range(out.shape[0]):
            out[leaf] = halves(halves_sum(nt(expand[leaf], jacobi[leaf])))


def ahead_kernel(m2l_list, m2l_type, table, packed, tiles, out, turned, first, sums):
    core = core_index()
    me = lax.axis_index("leaf")
    base = chip_base()
    rank = table.shape[2]

    @pl.when(core == 0)
    def _():
        for leaf in range(first.shape[0]):
            first[leaf] = nt(packed[leaf], tiles[leaf, 0])
            for k in range(turned.shape[1]):
                turned[leaf, k] = tiles[leaf, k + 1].T

    @pl.when(core == 1)
    def _():
        slots = jnp.bitwise_xor(m2l_list[...], me)
        kinds = m2l_type[...]
        sums[...] = jnp.zeros_like(sums)
        for k in range(m2l_list.shape[1]):
            slot, kind = slots[0, k], kinds[0, k]
            sums[slot, :rank] += table[base, kind].astype(F32)
            sums[slot, rank:] += table[base + 1, kind].astype(F32)
        for slot in range(out.shape[0]):
            out[slot] = halves(sums[slot])


def far_kernel(boxes, sources, near, m2m, apply, keep, send):
    core = core_index()
    leaves, rows = near.shape[:2]
    combos = rows // 2
    rank = m2m.shape[2]

    @pl.when(core == 0)
    def _():
        keep[...] = near[:, :combos]
        send[...] = near[:, combos:]

    @pl.when(core == 1)
    def _():
        local = None
        for slot in range(boxes.shape[0]):
            box = boxes[slot]
            part = nn(jnp.concatenate([box, box], axis=1), sources[slot])
            local = part if local is None else local + part
        local = local.astype(BF16)
        mask = by_channel(rows, combos, rank)
        down = []
        for leaf in range(leaves):
            trans = chip_m2m(m2m, leaf)
            down.append(jnp.where(mask, nt(local, trans), 0.0).astype(BF16))
        for leaf in range(leaves):
            far = nn(jnp.concatenate([down[leaf], down[leaf]], axis=1), apply[leaf])
            keep[leaf] = far[combos:]
            send[leaf] = far[:combos]


def final_kernel(live, keep, recv, out):
    total = (keep[...] + recv[...]) * live[...][:, None, :]
    out[...] = jnp.swapaxes(total, 0, 1)


def body(
    currents, counts, near_list, m2l_list, m2l_type, interp, compress, m2m, m2l, near_tiles, jacobi
):
    combos, leaves, unknowns = currents.shape
    nodes, rank = compress.shape[1:]
    rows = 2 * combos
    entries = m2l_list.shape[1]
    n = lax.axis_size("leaf")
    chans = lax.axis_size("chan")
    shape = jax.ShapeDtypeStruct

    def permute(value, target):
        moves = []
        for leaf in range(n):
            for chan in range(chans):
                to_leaf, to_chan = target(leaf, chan)
                moves.append((leaf * chans + chan, to_leaf * chans + to_chan))
        return lax.ppermute(value, ("leaf", "chan"), moves)

    def swap(value):
        return permute(value, lambda leaf, chan: (leaf, chan ^ 1))

    def first(leaf, chan):
        if chan % 2:
            return leaf ^ 1, chan
        if leaf in (0, n - 1):
            return leaf, chan ^ 2
        return (leaf + 1 if leaf % 2 else leaf - 1), chan

    def second(leaf, chan):
        return (leaf, chan ^ 2) if chan % 2 else (leaf ^ 1, chan)

    recv = swap(currents)
    interp_t = jnp.swapaxes(interp, 1, 2)
    comp_t = jnp.swapaxes(compress, 1, 2)
    mine, live = call(
        load_kernel,
        (shape((leaves, combos, unknowns), F32), shape((leaves, unknowns), F32)),
        [HBM] * 2,
        [
            pltpu.SMEM((leaves,), jnp.int32),
            pltpu.VMEM(currents.shape, BF16),
            pltpu.SemaphoreType.DMA((2,)),
        ],
    )(*in_hbm(counts, currents))
    packed, boxes = call(
        box_kernel,
        (shape((leaves + 1, rows, unknowns), BF16), shape((1, rows, 2 * rank), BF16)),
        [VMEM] * 6,
    )(mine, live, recv, interp_t, comp_t, m2m)
    double = shape((leaves, 4 * rank, unknowns), BF16)
    by_edge = permute(packed, first)
    comp_t, after = lax.optimization_barrier((comp_t, packed))
    expand = call(expand_kernel, double, [VMEM] * 2)(interp_t, comp_t)
    after, expand = lax.optimization_barrier((after, expand))
    by_pair = permute(after, second)
    m2l, expand = lax.optimization_barrier((m2l, expand))
    sources, turned, first_near = call(
        ahead_kernel,
        (
            shape((n, 4 * rank, rank), BF16),
            shape((leaves, AHEAD, unknowns, unknowns), BF16),
            shape((leaves, rows, unknowns), F32),
        ),
        [VMEM] * 5,
        [pltpu.VMEM((n, 2 * rank, rank), F32)],
    )(m2l_list, m2l_type, m2l, packed, near_tiles)
    boxes = jnp.concatenate([boxes, by_edge[leaves:, :, : 2 * rank]], axis=0)
    boxes, expand, sources = lax.optimization_barrier((boxes, expand, sources))
    apply = call(apply_kernel, double, [VMEM] * 2)(expand, jacobi)
    step = 2
    while step < n:
        boxes = jnp.concatenate(
            [
                boxes,
                permute(
                    boxes,
                    lambda leaf, chan, step=step: (leaf ^ step, chan) if chan % 2 else (leaf, chan ^ 2),
                ),
            ],
            axis=0,
        )
        step *= 2
    near = call(
        near_kernel,
        shape((leaves, rows, unknowns), F32),
        [VMEM] * 8,
        [pltpu.VMEM((3 * leaves, rows, unknowns), F32)],
    )(near_list, packed, by_pair, by_edge, near_tiles, turned, first_near, jacobi)
    part = shape((leaves, combos, unknowns), F32)
    keep, send = call(far_kernel, (part, part), [VMEM] * 5)(boxes, sources, near, m2m, apply)
    return call(final_kernel, shape(currents.shape, F32), [VMEM] * 3)(live, keep, swap(send))


def solution(mesh):
    placed = (
        P(("groups", "chan"), "leaf", None),
        P(("groups", "leaf")),
        P(("groups", "leaf"), None),
        P(("groups", "leaf"), None),
        P(("groups", "leaf"), None),
        P(("groups", "leaf"), None, None),
        P(),
        P(),
        P(),
        P(("groups", "leaf"), None, None, None),
        P(("groups", "leaf"), None, None),
    )
    return jax.shard_map(
        body,
        mesh=mesh,
        in_specs=placed,
        out_specs=P(("groups", "chan"), "leaf", None),
        check_vma=False,
    )
```

```python
import jax
import jax.numpy as jnp
from jax import lax
from jax.experimental import pallas as pl
from jax.experimental.pallas import tpu as pltpu
from jax.sharding import PartitionSpec as P

F32 = jnp.float32
BF16 = jnp.bfloat16
NT = (((1,), (1,)), ((), ()))
VMEM = pl.BlockSpec(memory_space=pltpu.VMEM)
HBM = pl.BlockSpec(memory_space=pltpu.HBM)
INC = 8
COST = 2 * 10**9
AHEAD = 2
KCOST = 2000000000
PCOST = 2000000000
NCOST = 1000000


def call(kernel, out_shape, in_specs, scratch=(), cost=COST):
    return pl.pallas_call(
        kernel,
        out_shape=out_shape,
        in_specs=in_specs,
        out_specs=jax.tree.map(lambda _: VMEM, out_shape),
        scratch_shapes=list(scratch),
        compiler_params=pltpu.CompilerParams(vmem_limit_bytes=16 << 20),
        cost_estimate=pl.CostEstimate(flops=cost, bytes_accessed=0, transcendentals=0),
    )


def in_hbm(*arrays):
    return [pltpu.with_memory_space_constraint(array, pltpu.HBM) for array in arrays]


def nt(a, b):
    return lax.dot_general(a, b, NT, preferred_element_type=F32)


def nn(a, b):
    return jnp.dot(a, b, preferred_element_type=F32)


def tn(a, b):
    return lax.dot_general(a, b, (((0,), (0,)), ((), ())), preferred_element_type=F32)


def halves(value):
    high = value.astype(BF16)
    return jnp.concatenate([high, (value - high.astype(F32)).astype(BF16)], axis=0)


def halves_sum(value):
    half = value.shape[0] // 2
    return value[:half] + value[half:]


def twice(value):
    return jnp.concatenate([value, value], axis=1)


def load_kernel(counts, own, mine, live, counts_s, own_s, sems):
    copies = [
        pltpu.make_async_copy(counts, counts_s, sems.at[0]),
        pltpu.make_async_copy(own, own_s, sems.at[1]),
    ]
    for copy in copies:
        copy.start()
    leaves, unknowns = live.shape
    slots = lax.broadcasted_iota(jnp.int32, (1, unknowns), 1)
    copies[0].wait()
    for leaf in range(leaves):
        live[leaf : leaf + 1] = jnp.where(slots < counts_s[leaf], 1.0, 0.0)
    copies[1].wait()
    mine[...] = jnp.swapaxes(own_s[...].astype(F32), 0, 1) * live[...][:, None, :]


def box_kernel(
    channel, mine, interp_t, comp_t, m2m, near_list, m2l_list, m2l_type, packed, box, places, slots, kinds
):
    me = lax.axis_index("leaf")
    count = lax.axis_size("leaf")
    places[...] = near_list[...] - (me - 1) * mine.shape[0]
    slots[...] = lax.rem(me - m2l_list[...] + count, count)
    kinds[...] = m2l_type[...]
    leaves, combos, unknowns = mine.shape
    rank = m2m.shape[2]
    x = mine[...].astype(BF16)
    packed[0:leaves] = x
    chan = channel()
    nodes = jnp.concatenate(
        [nt(x[leaf], interp_t[leaf]).astype(BF16) for leaf in range(leaves)], axis=0
    )
    moments = nt(nodes, comp_t[chan]).astype(BF16)
    total = None
    for leaf in range(leaves):
        part = nn(moments[leaf * combos : (leaf + 1) * combos], m2m[chan, leaf])
        total = part if total is None else total + part
    pair = twice(total).astype(BF16)
    packed[leaves] = jnp.concatenate(
        [pair, jnp.zeros((combos, unknowns - 2 * rank), BF16)], axis=1
    )
    box[0] = pair


def prepare_kernel(
    channel, packed, tiles, interp_t, comp_t, m2m, slots, kinds, jacobi, table,
    turned, first, apply, sources, expand, mats, sums, mat_sems,
):
    leaves = first.shape[0]
    chan = channel()
    kind = kinds[...]
    copies = [
        pltpu.make_async_copy(table.at[chan, kind[0, k]], mats.at[k], mat_sems.at[k])
        for k in range(mats.shape[0])
    ]
    for copy in copies:
        copy.start()
    comp = comp_t[chan]
    for leaf in range(leaves):
        expand[leaf] = halves(nn(comp, interp_t[leaf]))
    for leaf in range(leaves):
        first[leaf] = nt(packed[leaf], tiles[leaf, 0])
        for k in range(turned.shape[1]):
            turned[leaf, k] = tiles[leaf, k + 1].T
    applied = [halves(halves_sum(nt(expand[leaf], jacobi[leaf]))) for leaf in range(leaves)]
    for leaf in range(leaves):
        child = m2m[chan, leaf]
        apply[leaf] = halves(tn(jnp.concatenate([child, child], axis=0), applied[leaf]))
    for copy in copies:
        copy.wait()
    slot = slots[...]
    sums[...] = jnp.zeros_like(sums)
    for k in range(mats.shape[0]):
        sums[slot[0, k]] += mats[k].astype(F32)
    for place in range(sources.shape[0]):
        sources[place] = halves(sums[place])


def near_kernel(places, packed, high, low, tiles, turned, first, jacobi, near, beside):
    leaves, neighbours = places.shape
    ahead = turned.shape[1]
    places = places[...]
    beside[0:leaves] = low[0:leaves].astype(F32)
    beside[leaves : 2 * leaves] = packed[0:leaves].astype(F32)
    beside[2 * leaves : 3 * leaves] = high[0:leaves].astype(F32)
    sums = []
    for leaf in range(leaves):
        total = first[leaf]
        for k in range(1, neighbours):
            x = beside[places[leaf, k]].astype(BF16)
            if k <= ahead:
                total = total + nn(x, turned[leaf, k - 1])
            else:
                total = total + nt(x, tiles[leaf, k])
        sums.append(halves(total))
    for leaf in range(leaves):
        near[leaf] = halves_sum(nt(sums[leaf], jacobi[leaf]))


def final_kernel(sources, near, live, apply, box, high, low, *refs):
    *further, out = refs
    leaves, lanes = near.shape[0], box.shape[2]
    boxes = [box[0], low[leaves, :, :lanes]] + [ref[0] for ref in further] + [high[leaves, :, :lanes]]
    local = None
    for slot in range(sources.shape[0]):
        part = nn(boxes[slot], sources[slot])
        local = part if local is None else local + part
    local = twice(local).astype(BF16)
    for leaf in range(near.shape[0]):
        far = nn(local, apply[leaf])
        out[:, leaf, :] = (near[leaf] + far) * live[leaf : leaf + 1]


def body(
    currents, counts, near_list, m2l_list, m2l_type, interp, compress, m2m, m2l, near_tiles, jacobi
):
    combos, leaves, unknowns = currents.shape
    rank = compress.shape[2]
    entries = m2l_list.shape[1]
    n = lax.axis_size("leaf")
    chans = lax.axis_size("chan")
    shape = jax.ShapeDtypeStruct

    def channel():
        return lax.div(lax.axis_index("chan") * combos, INC)

    def bound(kernel):
        return lambda *refs: kernel(channel, *refs)

    def permute(value, shift, cross):
        moves = []
        for leaf in range(n):
            for chan in range(chans):
                to = (leaf + shift) % n * chans + (chan ^ 1 if cross else chan)
                moves.append((leaf * chans + chan, to))
        return lax.ppermute(value, ("leaf", "chan"), moves)

    interp_t = jnp.swapaxes(interp, 1, 2)
    comp_t = jnp.swapaxes(compress, 1, 2)
    part = shape((leaves, combos, unknowns), F32)
    mine, live = call(
        load_kernel,
        (part, shape((leaves, unknowns), F32)),
        [HBM] * 2,
        [
            pltpu.SMEM((leaves,), jnp.int32),
            pltpu.VMEM(currents.shape, BF16),
            pltpu.SemaphoreType.DMA((2,)),
        ],
    )(*in_hbm(counts, currents))
    packed, box, places, slots, kinds = call(
        bound(box_kernel),
        (
            shape((leaves + 1, combos, unknowns), BF16),
            shape((1, combos, 2 * rank), BF16),
            shape(near_list.shape, jnp.int32),
            shape(m2l_list.shape, jnp.int32),
            shape(m2l_type.shape, jnp.int32),
        ),
        [VMEM] * 7,
        cost=KCOST,
    )(mine, interp_t, comp_t, m2m, near_list, m2l_list, m2l_type)
    other = permute(box, 0, True)
    low = permute(packed, 1, False)

    high = permute(packed, -1, False)
    further = [permute(other, shift, True) for shift in range(2, n - 1)]
    after, _ = lax.optimization_barrier((packed, other))
    turned, first, apply, sources = call(
        bound(prepare_kernel),
        (
            shape((leaves, AHEAD, unknowns, unknowns), BF16),
            part,
            shape((leaves, 2 * rank, unknowns), BF16),
            shape((n, 2 * rank, rank), BF16),
        ),
        [VMEM] * 8 + [HBM],
        [
            pltpu.VMEM((leaves, 2 * rank, unknowns), BF16),
            pltpu.VMEM((entries, rank, rank), BF16),
            pltpu.VMEM((n, rank, rank), F32),
            pltpu.SemaphoreType.DMA((entries,)),
        ],
        PCOST,
    )(after, near_tiles, interp_t, comp_t, m2m, slots, kinds, jacobi, *in_hbm(m2l))
    near = call(
        near_kernel, part, [VMEM] * 8, [pltpu.VMEM((3 * leaves, combos, unknowns), F32)], NCOST
    )(places, packed, high, low, near_tiles, turned, first, jacobi)
    return call(final_kernel, shape(currents.shape, F32), [VMEM] * (7 + len(further)))(
        sources, near, live, apply, box, high, low, *further
    )


def solution(mesh):
    placed = (
        P(("groups", "chan"), "leaf", None),
        P(("groups", "leaf")),
        P(("groups", "leaf"), None),
        P(("groups", "leaf"), None),
        P(("groups", "leaf"), None),
        P(("groups", "leaf"), None, None),
        P(),
        P(),
        P(),
        P(("groups", "leaf"), None, None, None),
        P(("groups", "leaf"), None, None),
    )
    return jax.shard_map(
        body,
        mesh=mesh,
        in_specs=placed,
        out_specs=P(("groups", "chan"), "leaf", None),
        check_vma=False,
    )
```

```python
import jax
import jax.numpy as jnp
from jax import lax
from jax.experimental import pallas as pl
from jax.experimental.pallas import tpu as pltpu
from jax.sharding import PartitionSpec as P

F32 = jnp.float32
BF16 = jnp.bfloat16
NT = (((1,), (1,)), ((), ()))
VMEM = pl.BlockSpec(memory_space=pltpu.VMEM)
HBM = pl.BlockSpec(memory_space=pltpu.HBM)
INC = 8
COST = 2 * 10**9
AHEAD = 4
KCOST = 2000000000
PCOST = 2000000000
NCOST = 1000000


def call(kernel, out_shape, in_specs, scratch=(), cost=COST):
    return pl.pallas_call(
        kernel,
        out_shape=out_shape,
        in_specs=in_specs,
        out_specs=jax.tree.map(lambda _: VMEM, out_shape),
        scratch_shapes=list(scratch),
        compiler_params=pltpu.CompilerParams(vmem_limit_bytes=16 << 20),
        cost_estimate=pl.CostEstimate(flops=cost, bytes_accessed=0, transcendentals=0),
    )


def in_hbm(*arrays):
    return [pltpu.with_memory_space_constraint(array, pltpu.HBM) for array in arrays]


def nt(a, b):
    return lax.dot_general(a, b, NT, preferred_element_type=F32)


def nn(a, b):
    return jnp.dot(a, b, preferred_element_type=F32)


def tn(a, b):
    return lax.dot_general(a, b, (((0,), (0,)), ((), ())), preferred_element_type=F32)


def halves(value):
    high = value.astype(BF16)
    return jnp.concatenate([high, (value - high.astype(F32)).astype(BF16)], axis=0)


def halves_sum(value):
    half = value.shape[0] // 2
    return value[:half] + value[half:]


def twice(value):
    return jnp.concatenate([value, value], axis=1)


def load_kernel(
    channel, counts, own, comp_t, m2m, near_list, m2l_list, m2l_type,
    mine, live, comp_out, m2m_out, places, slots, kinds, counts_s, own_s, near_s, list_s, sems,
):
    chan = channel()
    me = lax.axis_index("leaf")
    count = lax.axis_size("leaf")
    pairs = (
        (counts, counts_s),
        (own, own_s),
        (comp_t.at[chan], comp_out),
        (m2m.at[chan], m2m_out),
        (near_list, near_s),
        (m2l_list, list_s),
        (m2l_type, kinds),
    )
    copies = [pltpu.make_async_copy(a, b, sems.at[k]) for k, (a, b) in enumerate(pairs)]
    for copy in copies:
        copy.start()
    leaves, unknowns = live.shape
    lanes = lax.broadcasted_iota(jnp.int32, (1, unknowns), 1)
    copies[0].wait()
    for leaf in range(leaves):
        live[leaf : leaf + 1] = jnp.where(lanes < counts_s[leaf], 1.0, 0.0)
    copies[1].wait()
    mine[...] = jnp.swapaxes(own_s[...].astype(F32), 0, 1) * live[...][:, None, :]
    for copy in copies[2:]:
        copy.wait()
    places[...] = near_s[...] - (me - 1) * leaves
    slots[...] = lax.rem(me - list_s[...] + count, count)


def box_kernel(mine, interp_t, comp_t, m2m, packed, box):
    leaves, combos, unknowns = mine.shape
    x = mine[...].astype(BF16)
    packed[0:leaves] = x
    nodes = jnp.concatenate(
        [nt(x[leaf], interp_t[leaf]).astype(BF16) for leaf in range(leaves)], axis=0
    )
    moments = nt(nodes, comp_t[...]).astype(BF16)
    total = None
    for leaf in range(leaves):
        part = nn(moments[leaf * combos : (leaf + 1) * combos], m2m[leaf])
        total = part if total is None else total + part
    pair = twice(total).astype(BF16)
    packed[leaves] = jnp.concatenate(
        [pair, jnp.zeros((combos, unknowns - pair.shape[1]), BF16)], axis=1
    )
    box[0] = pair


def prepare_kernel(
    channel, packed, tiles, interp_t, comp_t, m2m, slots, kinds, jacobi, table,
    turned, first, apply, sources, expand, mats, sums, mat_sems,
):
    leaves = first.shape[0]
    chan = channel()
    kind = kinds[...]
    copies = [
        pltpu.make_async_copy(table.at[chan, kind[0, k]], mats.at[k], mat_sems.at[k])
        for k in range(mats.shape[0])
    ]
    for copy in copies:
        copy.start()
    comp = comp_t[...]
    for leaf in range(leaves):
        expand[leaf] = halves(nn(comp, interp_t[leaf]))
    for leaf in range(leaves):
        first[leaf] = nt(packed[leaf], tiles[leaf, 0])
        for k in range(turned.shape[1]):
            turned[leaf, k] = tiles[leaf, k + 1].T
    applied = [halves(halves_sum(nt(expand[leaf], jacobi[leaf]))) for leaf in range(leaves)]
    for leaf in range(leaves):
        child = m2m[leaf]
        apply[leaf] = halves(tn(jnp.concatenate([child, child], axis=0), applied[leaf]))
    for copy in copies:
        copy.wait()
    slot = slots[...]
    sums[...] = jnp.zeros_like(sums)
    for k in range(mats.shape[0]):
        sums[slot[0, k]] += mats[k].astype(F32)
    for place in range(sources.shape[0]):
        sources[place] = halves(sums[place])


def near_kernel(places, packed, low, high, tiles, turned, first, jacobi, near, beside):
    leaves, neighbours = places.shape
    ahead = turned.shape[1]
    places = places[...]
    beside[0:leaves] = low[0:leaves].astype(F32)
    beside[leaves : 2 * leaves] = packed[0:leaves].astype(F32)
    beside[2 * leaves : 3 * leaves] = high[0:leaves].astype(F32)
    sums = []
    for leaf in range(leaves):
        total = first[leaf]
        for k in range(1, neighbours):
            x = beside[places[leaf, k]].astype(BF16)
            if k <= ahead:
                total = total + nn(x, turned[leaf, k - 1])
            else:
                total = total + nt(x, tiles[leaf, k])
        sums.append(halves(total))
    for leaf in range(leaves):
        near[leaf] = halves_sum(nt(sums[leaf], jacobi[leaf]))


def final_kernel(sources, near, live, apply, box, low, high, *refs):
    *further, out = refs
    leaves, lanes = near.shape[0], box.shape[2]
    boxes = [box[0], low[leaves, :, :lanes]] + [ref[0] for ref in further] + [high[leaves, :, :lanes]]
    local = None
    for slot in range(sources.shape[0]):
        part = nn(boxes[slot], sources[slot])
        local = part if local is None else local + part
    local = twice(local).astype(BF16)
    for leaf in range(near.shape[0]):
        far = nn(local, apply[leaf])
        out[:, leaf, :] = (near[leaf] + far) * live[leaf : leaf + 1]


def body(
    currents, counts, near_list, m2l_list, m2l_type, interp, compress, m2m, m2l, near_tiles, jacobi
):
    combos, leaves, unknowns = currents.shape
    rank = compress.shape[2]
    entries = m2l_list.shape[1]
    n = lax.axis_size("leaf")
    chans = lax.axis_size("chan")
    shape = jax.ShapeDtypeStruct

    def channel():
        return lax.div(lax.axis_index("chan") * combos, INC)

    def bound(kernel):
        return lambda *refs: kernel(channel, *refs)

    def permute(value, shift, cross):
        moves = []
        for leaf in range(n):
            for chan in range(chans):
                to = (leaf + shift) % n * chans + (chan ^ 1 if cross else chan)
                moves.append((leaf * chans + chan, to))
        return lax.ppermute(value, ("leaf", "chan"), moves)

    interp_t = jnp.swapaxes(interp, 1, 2)
    comp_t = jnp.swapaxes(compress, 1, 2)
    part = shape((leaves, combos, unknowns), F32)
    nodes = interp_t.shape[1]
    mine, live, comp_v, m2m_v, places, slots, kinds = call(
        bound(load_kernel),
        (
            part,
            shape((leaves, unknowns), F32),
            shape((rank, nodes), BF16),
            shape((leaves, rank, rank), BF16),
            shape(near_list.shape, jnp.int32),
            shape(m2l_list.shape, jnp.int32),
            shape(m2l_type.shape, jnp.int32),
        ),
        [HBM] * 7,
        [
            pltpu.SMEM((leaves,), jnp.int32),
            pltpu.VMEM(currents.shape, BF16),
            pltpu.VMEM(near_list.shape, jnp.int32),
            pltpu.VMEM(m2l_list.shape, jnp.int32),
            pltpu.SemaphoreType.DMA((7,)),
        ],
    )(*in_hbm(counts, currents, comp_t, m2m, near_list, m2l_list, m2l_type))
    packed, box = call(
        box_kernel,
        (shape((leaves + 1, combos, unknowns), BF16), shape((1, combos, 2 * rank), BF16)),
        [VMEM] * 4,
        cost=KCOST,
    )(mine, interp_t, comp_v, m2m_v)
    other = permute(box, 0, True)
    low = permute(packed, 1, False)

    high = permute(packed, -1, False)
    further = [permute(other, shift, True) for shift in range(2, n - 1)]
    after, _ = lax.optimization_barrier((packed, other))
    turned, first, apply, sources = call(
        bound(prepare_kernel),
        (
            shape((leaves, AHEAD, unknowns, unknowns), BF16),
            part,
            shape((leaves, 2 * rank, unknowns), BF16),
            shape((n, 2 * rank, rank), BF16),
        ),
        [VMEM] * 8 + [HBM],
        [
            pltpu.VMEM((leaves, 2 * rank, unknowns), BF16),
            pltpu.VMEM((entries, rank, rank), BF16),
            pltpu.VMEM((n, rank, rank), F32),
            pltpu.SemaphoreType.DMA((entries,)),
        ],
        PCOST,
    )(after, near_tiles, interp_t, comp_v, m2m_v, slots, kinds, jacobi, *in_hbm(m2l))
    near = call(
        near_kernel, part, [VMEM] * 8, [pltpu.VMEM((3 * leaves, combos, unknowns), F32)], NCOST
    )(places, packed, low, high, near_tiles, turned, first, jacobi)
    return call(final_kernel, shape(currents.shape, F32), [VMEM] * (7 + len(further)))(
        sources, near, live, apply, box, low, high, *further
    )


def solution(mesh):
    placed = (
        P(("groups", "chan"), "leaf", None),
        P(("groups", "leaf")),
        P(("groups", "leaf"), None),
        P(("groups", "leaf"), None),
        P(("groups", "leaf"), None),
        P(("groups", "leaf"), None, None),
        P(),
        P(),
        P(),
        P(("groups", "leaf"), None, None, None),
        P(("groups", "leaf"), None, None),
    )
    return jax.shard_map(
        body,
        mesh=mesh,
        in_specs=placed,
        out_specs=P(("groups", "chan"), "leaf", None),
        check_vma=False,
    )
```

```python
import jax
import jax.numpy as jnp
from jax import lax
from jax.experimental import pallas as pl
from jax.experimental.pallas import tpu as pltpu
from jax.sharding import PartitionSpec as P

F32 = jnp.float32
BF16 = jnp.bfloat16
NT = (((1,), (1,)), ((), ()))
VMEM = pl.BlockSpec(memory_space=pltpu.VMEM)
HBM = pl.BlockSpec(memory_space=pltpu.HBM)
INC = 8
COST = 2 * 10**9
AHEAD = 4
KCOST = 2000000000
PCOST = 2000000000
NCOST = 1000000


def call(kernel, out_shape, in_specs, scratch=(), cost=COST):
    return pl.pallas_call(
        kernel,
        out_shape=out_shape,
        in_specs=in_specs,
        out_specs=jax.tree.map(lambda _: VMEM, out_shape),
        scratch_shapes=list(scratch),
        compiler_params=pltpu.CompilerParams(vmem_limit_bytes=16 << 20),
        cost_estimate=pl.CostEstimate(flops=cost, bytes_accessed=0, transcendentals=0),
    )


def in_hbm(*arrays):
    return [pltpu.with_memory_space_constraint(array, pltpu.HBM) for array in arrays]


def nt(a, b):
    return lax.dot_general(a, b, NT, preferred_element_type=F32)


def nn(a, b):
    return jnp.dot(a, b, preferred_element_type=F32)


def tn(a, b):
    return lax.dot_general(a, b, (((0,), (0,)), ((), ())), preferred_element_type=F32)


def halves(value):
    high = value.astype(BF16)
    return jnp.concatenate([high, (value - high.astype(F32)).astype(BF16)], axis=0)


def halves_sum(value):
    half = value.shape[0] // 2
    return value[:half] + value[half:]


def twice(value):
    return jnp.concatenate([value, value], axis=1)


def load_kernel(
    channel, counts, own, comp_t, m2m, near_list, m2l_list, m2l_type,
    mine, live, comp_out, m2m_out, places, slots, kinds, counts_s, own_s, near_s, list_s, sems,
):
    chan = channel()
    me = lax.axis_index("leaf")
    count = lax.axis_size("leaf")
    pairs = (
        (counts, counts_s),
        (own, own_s),
        (comp_t.at[chan], comp_out),
        (m2m.at[chan], m2m_out),
        (near_list, near_s),
        (m2l_list, list_s),
        (m2l_type, kinds),
    )
    copies = [pltpu.make_async_copy(a, b, sems.at[k]) for k, (a, b) in enumerate(pairs)]
    for copy in copies:
        copy.start()
    leaves, unknowns = live.shape
    lanes = lax.broadcasted_iota(jnp.int32, (1, unknowns), 1)
    copies[0].wait()
    for leaf in range(leaves):
        live[leaf : leaf + 1] = jnp.where(lanes < counts_s[leaf], 1.0, 0.0)
    copies[1].wait()
    mine[...] = jnp.swapaxes(own_s[...].astype(F32), 0, 1) * live[...][:, None, :]
    for copy in copies[2:]:
        copy.wait()
    places[...] = near_s[...] - (me - 1) * leaves
    slots[...] = lax.rem(me - list_s[...] + count, count)


def box_kernel(mine, interp_t, comp_t, m2m, packed, box):
    leaves, combos, unknowns = mine.shape
    x = mine[...].astype(BF16)
    packed[0:leaves] = x
    nodes = jnp.concatenate(
        [nt(x[leaf], interp_t[leaf]).astype(BF16) for leaf in range(leaves)], axis=0
    )
    moments = nt(nodes, comp_t[...]).astype(BF16)
    total = None
    for leaf in range(leaves):
        part = nn(moments[leaf * combos : (leaf + 1) * combos], m2m[leaf])
        total = part if total is None else total + part
    pair = twice(total).astype(BF16)
    packed[leaves] = jnp.concatenate(
        [pair, jnp.zeros((combos, unknowns - pair.shape[1]), BF16)], axis=1
    )
    box[0] = pair


def prepare_kernel(
    channel, packed, tiles, interp_t, comp_t, m2m, slots, kinds, jacobi, table,
    turned, first, apply, sources, expand, mats, sums, mat_sems,
):
    leaves = first.shape[0]
    chan = channel()
    kind = kinds[...]
    copies = [
        pltpu.make_async_copy(table.at[chan, kind[0, k]], mats.at[k], mat_sems.at[k])
        for k in range(mats.shape[0])
    ]
    for copy in copies:
        copy.start()
    comp = comp_t[...]
    for leaf in range(leaves):
        expand[leaf] = halves(nn(comp, interp_t[leaf]))
    for leaf in range(leaves):
        first[leaf] = nt(packed[leaf], tiles[leaf, 0])
        for k in range(turned.shape[1]):
            turned[leaf, k] = tiles[leaf, k + 1].T
    applied = [halves(halves_sum(nt(expand[leaf], jacobi[leaf]))) for leaf in range(leaves)]
    for leaf in range(leaves):
        child = m2m[leaf]
        apply[leaf] = halves(tn(jnp.concatenate([child, child], axis=0), applied[leaf]))
    for copy in copies:
        copy.wait()
    slot = slots[...]
    sums[...] = jnp.zeros_like(sums)
    for k in range(mats.shape[0]):
        sums[slot[0, k]] += mats[k].astype(F32)
    for place in range(sources.shape[0]):
        sources[place] = halves(sums[place])


def near_kernel(places, packed, low, high, tiles, turned, first, jacobi, near, beside):
    leaves, neighbours = places.shape
    ahead = turned.shape[1]
    places = places[...]
    beside[0:leaves] = low[0:leaves].astype(F32)
    beside[leaves : 2 * leaves] = packed[0:leaves].astype(F32)
    beside[2 * leaves : 3 * leaves] = high[0:leaves].astype(F32)
    sums = []
    for leaf in range(leaves):
        total = first[leaf]
        for k in range(1, neighbours):
            x = beside[places[leaf, k]].astype(BF16)
            if k <= ahead:
                total = total + nn(x, turned[leaf, k - 1])
            else:
                total = total + nt(x, tiles[leaf, k])
        sums.append(halves(total))
    for leaf in range(leaves):
        near[leaf] = halves_sum(nt(sums[leaf], jacobi[leaf]))


def final_kernel(sources, near, live, apply, box, low, high, *refs):
    *further, out = refs
    leaves, lanes = near.shape[0], box.shape[2]
    boxes = [box[0], low[leaves, :, :lanes]] + [ref[0] for ref in further] + [high[leaves, :, :lanes]]
    local = nn(jnp.concatenate(boxes, axis=1), sources[...].reshape(-1, sources.shape[2]))
    local = twice(local).astype(BF16)
    done = [(near[leaf] + nn(local, apply[leaf])) * live[leaf : leaf + 1] for leaf in range(near.shape[0])]
    out[...] = jnp.swapaxes(jnp.stack(done), 0, 1)


def body(
    currents, counts, near_list, m2l_list, m2l_type, interp, compress, m2m, m2l, near_tiles, jacobi
):
    combos, leaves, unknowns = currents.shape
    rank = compress.shape[2]
    entries = m2l_list.shape[1]
    n = lax.axis_size("leaf")
    chans = lax.axis_size("chan")
    shape = jax.ShapeDtypeStruct

    def channel():
        return lax.div(lax.axis_index("chan") * combos, INC)

    def bound(kernel):
        return lambda *refs: kernel(channel, *refs)

    def permute(value, shift, cross):
        moves = []
        for leaf in range(n):
            for chan in range(chans):
                to = (leaf + shift) % n * chans + (chan ^ 1 if cross else chan)
                moves.append((leaf * chans + chan, to))
        return lax.ppermute(value, ("leaf", "chan"), moves)

    interp_t = jnp.swapaxes(interp, 1, 2)
    comp_t = jnp.swapaxes(compress, 1, 2)
    part = shape((leaves, combos, unknowns), F32)
    nodes = interp_t.shape[1]
    mine, live, comp_v, m2m_v, places, slots, kinds = call(
        bound(load_kernel),
        (
            part,
            shape((leaves, unknowns), F32),
            shape((rank, nodes), BF16),
            shape((leaves, rank, rank), BF16),
            shape(near_list.shape, jnp.int32),
            shape(m2l_list.shape, jnp.int32),
            shape(m2l_type.shape, jnp.int32),
        ),
        [HBM] * 7,
        [
            pltpu.SMEM((leaves,), jnp.int32),
            pltpu.VMEM(currents.shape, BF16),
            pltpu.VMEM(near_list.shape, jnp.int32),
            pltpu.VMEM(m2l_list.shape, jnp.int32),
            pltpu.SemaphoreType.DMA((7,)),
        ],
    )(*in_hbm(counts, currents, comp_t, m2m, near_list, m2l_list, m2l_type))
    packed, box = call(
        box_kernel,
        (shape((leaves + 1, combos, unknowns), BF16), shape((1, combos, 2 * rank), BF16)),
        [VMEM] * 4,
        cost=KCOST,
    )(mine, interp_t, comp_v, m2m_v)
    other = permute(box, 0, True)
    low = permute(packed, 1, False)

    high = permute(packed, -1, False)
    further = [permute(other, shift, True) for shift in range(2, n - 1)]
    after, _ = lax.optimization_barrier((packed, other))
    turned, first, apply, sources = call(
        bound(prepare_kernel),
        (
            shape((leaves, AHEAD, unknowns, unknowns), BF16),
            part,
            shape((leaves, 2 * rank, unknowns), BF16),
            shape((n, 2 * rank, rank), BF16),
        ),
        [VMEM] * 8 + [HBM],
        [
            pltpu.VMEM((leaves, 2 * rank, unknowns), BF16),
            pltpu.VMEM((entries, rank, rank), BF16),
            pltpu.VMEM((n, rank, rank), F32),
            pltpu.SemaphoreType.DMA((entries,)),
        ],
        PCOST,
    )(after, near_tiles, interp_t, comp_v, m2m_v, slots, kinds, jacobi, *in_hbm(m2l))
    near = call(
        near_kernel, part, [VMEM] * 8, [pltpu.VMEM((3 * leaves, combos, unknowns), F32)], NCOST
    )(places, packed, low, high, near_tiles, turned, first, jacobi)
    return call(final_kernel, shape(currents.shape, F32), [VMEM] * (7 + len(further)))(
        sources, near, live, apply, box, low, high, *further
    )


def solution(mesh):
    placed = (
        P(("groups", "chan"), "leaf", None),
        P(("groups", "leaf")),
        P(("groups", "leaf"), None),
        P(("groups", "leaf"), None),
        P(("groups", "leaf"), None),
        P(("groups", "leaf"), None, None),
        P(),
        P(),
        P(),
        P(("groups", "leaf"), None, None, None),
        P(("groups", "leaf"), None, None),
    )
    return jax.shard_map(
        body,
        mesh=mesh,
        in_specs=placed,
        out_specs=P(("groups", "chan"), "leaf", None),
        check_vma=False,
    )
```

```python
import jax
import jax.numpy as jnp
from jax import lax
from jax.experimental import pallas as pl
from jax.experimental.pallas import tpu as pltpu
from jax.sharding import PartitionSpec as P

F32 = jnp.float32
BF16 = jnp.bfloat16
NT = (((1,), (1,)), ((), ()))
VMEM = pl.BlockSpec(memory_space=pltpu.VMEM)
HBM = pl.BlockSpec(memory_space=pltpu.HBM)
INC = 8
COST = 2 * 10**9
AHEAD = 4
KCOST = 2000000000
PCOST = 2000000000
NCOST = 1000000


def call(kernel, out_shape, in_specs, scratch=(), cost=COST):
    return pl.pallas_call(
        kernel,
        out_shape=out_shape,
        in_specs=in_specs,
        out_specs=jax.tree.map(lambda _: VMEM, out_shape),
        scratch_shapes=list(scratch),
        compiler_params=pltpu.CompilerParams(vmem_limit_bytes=16 << 20),
        cost_estimate=pl.CostEstimate(flops=cost, bytes_accessed=0, transcendentals=0),
    )


def in_hbm(*arrays):
    return [pltpu.with_memory_space_constraint(array, pltpu.HBM) for array in arrays]


def nt(a, b):
    return lax.dot_general(a, b, NT, preferred_element_type=F32)


def nn(a, b):
    return jnp.dot(a, b, preferred_element_type=F32)


def tn(a, b):
    return lax.dot_general(a, b, (((0,), (0,)), ((), ())), preferred_element_type=F32)


def halves(value):
    high = value.astype(BF16)
    return jnp.concatenate([high, (value - high.astype(F32)).astype(BF16)], axis=0)


def halves_sum(value):
    half = value.shape[0] // 2
    return value[:half] + value[half:]


def twice(value):
    return jnp.concatenate([value, value], axis=1)


def load_kernel(
    channel, counts, own, comp_t, m2m, near_list, m2l_list, m2l_type,
    mine, live, comp_out, m2m_out, places, slots, kinds, counts_s, own_s, near_s, list_s, sems,
):
    chan = channel()
    me = lax.axis_index("leaf")
    count = lax.axis_size("leaf")
    pairs = (
        (counts, counts_s),
        (own, own_s),
        (comp_t.at[chan], comp_out),
        (m2m.at[chan], m2m_out),
        (near_list, near_s),
        (m2l_list, list_s),
        (m2l_type, kinds),
    )
    copies = [pltpu.make_async_copy(a, b, sems.at[k]) for k, (a, b) in enumerate(pairs)]
    for copy in copies:
        copy.start()
    leaves, unknowns = live.shape
    lanes = lax.broadcasted_iota(jnp.int32, (1, unknowns), 1)
    copies[0].wait()
    for leaf in range(leaves):
        live[leaf : leaf + 1] = jnp.where(lanes < counts_s[leaf], 1.0, 0.0)
    copies[1].wait()
    mine[...] = jnp.swapaxes(own_s[...].astype(F32), 0, 1) * live[...][:, None, :]
    for copy in copies[2:]:
        copy.wait()
    places[...] = near_s[...] - (me - 1) * leaves
    slots[...] = lax.rem(me - list_s[...] + count, count)


def box_kernel(mine, interp_t, comp_t, m2m, packed, box):
    leaves, combos, unknowns = mine.shape
    x = mine[...].astype(BF16)
    packed[0:leaves] = x
    nodes = jnp.concatenate(
        [nt(x[leaf], interp_t[leaf]).astype(BF16) for leaf in range(leaves)], axis=0
    )
    moments = nt(nodes, comp_t[...]).astype(BF16)
    total = None
    for leaf in range(leaves):
        part = nn(moments[leaf * combos : (leaf + 1) * combos], m2m[leaf])
        total = part if total is None else total + part
    pair = twice(total).astype(BF16)
    packed[leaves] = jnp.concatenate(
        [pair, jnp.zeros((combos, unknowns - pair.shape[1]), BF16)], axis=1
    )
    box[0] = pair


def prepare_kernel(
    channel, packed, tiles, interp_t, comp_t, m2m, slots, kinds, jacobi, table,
    turned, first, apply, back, sources, expand, mats, sums, mat_sems,
):
    leaves = first.shape[0]
    chan = channel()
    kind = kinds[...]
    copies = [
        pltpu.make_async_copy(table.at[chan, kind[0, k]], mats.at[k], mat_sems.at[k])
        for k in range(mats.shape[0])
    ]
    for copy in copies:
        copy.start()
    comp = comp_t[...]
    for leaf in range(leaves):
        top = jnp.max(jnp.abs(jacobi[leaf]).astype(F32), axis=(0, 1), keepdims=True)
        scale = jnp.where(top > 2.0**90, 2.0**-30, jnp.where(top < 2.0**-90, 2.0**30, 1.0))
        back[leaf : leaf + 1] = jnp.broadcast_to(1.0 / scale, (1, back.shape[1]))
        expand[leaf] = halves(nn(comp, interp_t[leaf]) * scale)
    for leaf in range(leaves):
        first[leaf] = nt(packed[leaf], tiles[leaf, 0])
        for k in range(turned.shape[1]):
            turned[leaf, k] = tiles[leaf, k + 1].T
    applied = [halves(halves_sum(nt(expand[leaf], jacobi[leaf]))) for leaf in range(leaves)]
    for leaf in range(leaves):
        child = m2m[leaf]
        apply[leaf] = halves(tn(jnp.concatenate([child, child], axis=0), applied[leaf]))
    for copy in copies:
        copy.wait()
    slot = slots[...]
    sums[...] = jnp.zeros_like(sums)
    for k in range(mats.shape[0]):
        sums[slot[0, k]] += mats[k].astype(F32)
    for place in range(sources.shape[0]):
        sources[place] = halves(sums[place])


def near_kernel(places, packed, low, high, tiles, turned, first, jacobi, near, beside):
    leaves, neighbours = places.shape
    ahead = turned.shape[1]
    places = places[...]
    beside[0:leaves] = low[0:leaves].astype(F32)
    beside[leaves : 2 * leaves] = packed[0:leaves].astype(F32)
    beside[2 * leaves : 3 * leaves] = high[0:leaves].astype(F32)
    sums = []
    for leaf in range(leaves):
        total = first[leaf]
        for k in range(1, neighbours):
            x = beside[places[leaf, k]].astype(BF16)
            if k <= ahead:
                total = total + nn(x, turned[leaf, k - 1])
            else:
                total = total + nt(x, tiles[leaf, k])
        sums.append(halves(total))
    for leaf in range(leaves):
        near[leaf] = halves_sum(nt(sums[leaf], jacobi[leaf]))


def final_kernel(sources, near, live, back, apply, box, low, high, *refs):
    *further, out = refs
    leaves, lanes = near.shape[0], box.shape[2]
    boxes = [box[0], low[leaves, :, :lanes]] + [ref[0] for ref in further] + [high[leaves, :, :lanes]]
    local = nn(jnp.concatenate(boxes, axis=1), sources[...].reshape(-1, sources.shape[2]))
    local = twice(local).astype(BF16)
    done = []
    for leaf in range(leaves):
        row = slice(leaf, leaf + 1)
        done.append((near[leaf] + nn(local, apply[leaf]) * back[row]) * live[row])
    out[...] = jnp.swapaxes(jnp.stack(done), 0, 1)


def body(
    currents, counts, near_list, m2l_list, m2l_type, interp, compress, m2m, m2l, near_tiles, jacobi
):
    combos, leaves, unknowns = currents.shape
    rank = compress.shape[2]
    entries = m2l_list.shape[1]
    n = lax.axis_size("leaf")
    chans = lax.axis_size("chan")
    shape = jax.ShapeDtypeStruct

    def channel():
        return lax.div(lax.axis_index("chan") * combos, INC)

    def bound(kernel):
        return lambda *refs: kernel(channel, *refs)

    def permute(value, shift, cross):
        moves = []
        for leaf in range(n):
            for chan in range(chans):
                to = (leaf + shift) % n * chans + (chan ^ 1 if cross else chan)
                moves.append((leaf * chans + chan, to))
        return lax.ppermute(value, ("leaf", "chan"), moves)

    interp_t = jnp.swapaxes(interp, 1, 2)
    comp_t = jnp.swapaxes(compress, 1, 2)
    part = shape((leaves, combos, unknowns), F32)
    nodes = interp_t.shape[1]
    mine, live, comp_v, m2m_v, places, slots, kinds = call(
        bound(load_kernel),
        (
            part,
            shape((leaves, unknowns), F32),
            shape((rank, nodes), BF16),
            shape((leaves, rank, rank), BF16),
            shape(near_list.shape, jnp.int32),
            shape(m2l_list.shape, jnp.int32),
            shape(m2l_type.shape, jnp.int32),
        ),
        [HBM] * 7,
        [
            pltpu.SMEM((leaves,), jnp.int32),
            pltpu.VMEM(currents.shape, BF16),
            pltpu.VMEM(near_list.shape, jnp.int32),
            pltpu.VMEM(m2l_list.shape, jnp.int32),
            pltpu.SemaphoreType.DMA((7,)),
        ],
    )(*in_hbm(counts, currents, comp_t, m2m, near_list, m2l_list, m2l_type))
    packed, box = call(
        box_kernel,
        (shape((leaves + 1, combos, unknowns), BF16), shape((1, combos, 2 * rank), BF16)),
        [VMEM] * 4,
        cost=KCOST,
    )(mine, interp_t, comp_v, m2m_v)
    other = permute(box, 0, True)
    low = permute(packed, 1, False)

    high = permute(packed, -1, False)
    further = [permute(other, shift, True) for shift in range(2, n - 1)]
    after, _ = lax.optimization_barrier((packed, other))
    turned, first, apply, back, sources = call(
        bound(prepare_kernel),
        (
            shape((leaves, AHEAD, unknowns, unknowns), BF16),
            part,
            shape((leaves, 2 * rank, unknowns), BF16),
            shape((leaves, unknowns), F32),
            shape((n, 2 * rank, rank), BF16),
        ),
        [VMEM] * 8 + [HBM],
        [
            pltpu.VMEM((leaves, 2 * rank, unknowns), BF16),
            pltpu.VMEM((entries, rank, rank), BF16),
            pltpu.VMEM((n, rank, rank), F32),
            pltpu.SemaphoreType.DMA((entries,)),
        ],
        PCOST,
    )(after, near_tiles, interp_t, comp_v, m2m_v, slots, kinds, jacobi, *in_hbm(m2l))
    near = call(
        near_kernel, part, [VMEM] * 8, [pltpu.VMEM((3 * leaves, combos, unknowns), F32)], NCOST
    )(places, packed, low, high, near_tiles, turned, first, jacobi)
    return call(final_kernel, shape(currents.shape, F32), [VMEM] * (8 + len(further)))(
        sources, near, live, back, apply, box, low, high, *further
    )


def solution(mesh):
    placed = (
        P(("groups", "chan"), "leaf", None),
        P(("groups", "leaf")),
        P(("groups", "leaf"), None),
        P(("groups", "leaf"), None),
        P(("groups", "leaf"), None),
        P(("groups", "leaf"), None, None),
        P(),
        P(),
        P(),
        P(("groups", "leaf"), None, None, None),
        P(("groups", "leaf"), None, None),
    )
    return jax.shard_map(
        body,
        mesh=mesh,
        in_specs=placed,
        out_specs=P(("groups", "chan"), "leaf", None),
        check_vma=False,
    )
```

```python
import jax
import jax.numpy as jnp
from jax import lax
from jax.experimental import pallas as pl
from jax.experimental.pallas import tpu as pltpu
from jax.sharding import PartitionSpec as P

F32 = jnp.float32
BF16 = jnp.bfloat16
NT = (((1,), (1,)), ((), ()))
VMEM = pl.BlockSpec(memory_space=pltpu.VMEM)
HBM = pl.BlockSpec(memory_space=pltpu.HBM)
INC = 8
COST = 2 * 10**9
AHEAD = 4
KCOST = 2000000000
PCOST = 2000000000
NCOST = 1000000


def call(kernel, out_shape, in_specs, scratch=(), cost=COST):
    return pl.pallas_call(
        kernel,
        out_shape=out_shape,
        in_specs=in_specs,
        out_specs=jax.tree.map(lambda _: VMEM, out_shape),
        scratch_shapes=list(scratch),
        compiler_params=pltpu.CompilerParams(vmem_limit_bytes=16 << 20),
        cost_estimate=pl.CostEstimate(flops=cost, bytes_accessed=0, transcendentals=0),
    )


def in_hbm(*arrays):
    return [pltpu.with_memory_space_constraint(array, pltpu.HBM) for array in arrays]


def nt(a, b):
    return lax.dot_general(a, b, NT, preferred_element_type=F32)


def nn(a, b):
    return jnp.dot(a, b, preferred_element_type=F32)


def tn(a, b):
    return lax.dot_general(a, b, (((0,), (0,)), ((), ())), preferred_element_type=F32)


def halves(value):
    high = value.astype(BF16)
    return jnp.concatenate([high, (value - high.astype(F32)).astype(BF16)], axis=0)


def halves_sum(value):
    half = value.shape[0] // 2
    return value[:half] + value[half:]


def twice(value):
    return jnp.concatenate([value, value], axis=1)


def load_kernel(
    channel, counts, own, comp_t, m2m, near_list, m2l_list, m2l_type,
    mine, live, comp_out, m2m_out, places, slots, kinds, counts_s, own_s, near_s, list_s, sems,
):
    chan = channel()
    me = lax.axis_index("leaf")
    count = lax.axis_size("leaf")
    pairs = (
        (counts, counts_s),
        (own, own_s),
        (comp_t.at[chan], comp_out),
        (m2m.at[chan], m2m_out),
        (near_list, near_s),
        (m2l_list, list_s),
        (m2l_type, kinds),
    )
    copies = [pltpu.make_async_copy(a, b, sems.at[k]) for k, (a, b) in enumerate(pairs)]
    for copy in copies:
        copy.start()
    leaves, unknowns = live.shape
    lanes = lax.broadcasted_iota(jnp.int32, (1, unknowns), 1)
    copies[0].wait()
    for leaf in range(leaves):
        live[leaf : leaf + 1] = jnp.where(lanes < counts_s[leaf], 1.0, 0.0)
    copies[1].wait()
    mine[...] = jnp.swapaxes(own_s[...].astype(F32), 0, 1) * live[...][:, None, :]
    for copy in copies[2:]:
        copy.wait()
    places[...] = near_s[...] - (me - 1) * leaves
    slots[...] = lax.rem(me - list_s[...] + count, count)


def box_kernel(mine, interp_t, comp_t, m2m, packed, box):
    leaves, combos, unknowns = mine.shape
    x = mine[...].astype(BF16)
    packed[0:leaves] = x
    nodes = jnp.concatenate(
        [nt(x[leaf], interp_t[leaf]).astype(BF16) for leaf in range(leaves)], axis=0
    )
    moments = nt(nodes, comp_t[...]).astype(BF16)
    total = None
    for leaf in range(leaves):
        part = nn(moments[leaf * combos : (leaf + 1) * combos], m2m[leaf])
        total = part if total is None else total + part
    pair = twice(total).astype(BF16)
    packed[leaves] = jnp.concatenate(
        [pair, jnp.zeros((combos, unknowns - pair.shape[1]), BF16)], axis=1
    )
    box[0] = pair


def prepare_kernel(
    channel, packed, tiles, interp_t, comp_t, m2m, slots, kinds, jacobi, table,
    turned, first, apply, back, sources, expand, mats, sums, mat_sems,
):
    leaves = first.shape[0]
    chan = channel()
    kind = kinds[...]
    copies = [
        pltpu.make_async_copy(table.at[chan, kind[0, k]], mats.at[k], mat_sems.at[k])
        for k in range(mats.shape[0])
    ]
    for copy in copies:
        copy.start()
    comp = comp_t[...]
    tops = [jnp.max(jnp.abs(jacobi[leaf]), axis=0, keepdims=True).astype(F32) for leaf in range(leaves)]
    top = jnp.max(jnp.concatenate(tops, axis=0), axis=1, keepdims=True)
    scale = jnp.where(top > 2.0**90, 2.0**-30, jnp.where(top < 2.0**-90, 2.0**30, 1.0))
    back[...] = jnp.broadcast_to(1.0 / scale, back.shape)
    for leaf in range(leaves):
        expand[leaf] = halves(nn(comp, interp_t[leaf]) * scale[leaf : leaf + 1])
    for leaf in range(leaves):
        first[leaf] = nt(packed[leaf], tiles[leaf, 0])
        for k in range(turned.shape[1]):
            turned[leaf, k] = tiles[leaf, k + 1].T
    applied = [halves(halves_sum(nt(expand[leaf], jacobi[leaf]))) for leaf in range(leaves)]
    for leaf in range(leaves):
        child = m2m[leaf]
        apply[leaf] = halves(tn(jnp.concatenate([child, child], axis=0), applied[leaf]))
    for copy in copies:
        copy.wait()
    slot = slots[...]
    sums[...] = jnp.zeros_like(sums)
    for k in range(mats.shape[0]):
        sums[slot[0, k]] += mats[k].astype(F32)
    for place in range(sources.shape[0]):
        sources[place] = halves(sums[place])


def near_kernel(places, packed, low, high, tiles, turned, first, jacobi, near, beside):
    leaves, neighbours = places.shape
    ahead = turned.shape[1]
    places = places[...]
    beside[0:leaves] = low[0:leaves].astype(F32)
    beside[leaves : 2 * leaves] = packed[0:leaves].astype(F32)
    beside[2 * leaves : 3 * leaves] = high[0:leaves].astype(F32)
    sums = []
    for leaf in range(leaves):
        total = first[leaf]
        for k in range(1, neighbours):
            x = beside[places[leaf, k]].astype(BF16)
            if k <= ahead:
                total = total + nn(x, turned[leaf, k - 1])
            else:
                total = total + nt(x, tiles[leaf, k])
        sums.append(halves(total))
    for leaf in range(leaves):
        near[leaf] = halves_sum(nt(sums[leaf], jacobi[leaf]))


def final_kernel(sources, near, live, back, apply, box, low, high, *refs):
    *further, out = refs
    leaves, lanes = near.shape[0], box.shape[2]
    boxes = [box[0], low[leaves, :, :lanes]] + [ref[0] for ref in further] + [high[leaves, :, :lanes]]
    local = nn(jnp.concatenate(boxes, axis=1), sources[...].reshape(-1, sources.shape[2]))
    local = twice(local).astype(BF16)
    done = []
    for leaf in range(leaves):
        row = slice(leaf, leaf + 1)
        done.append((near[leaf] + nn(local, apply[leaf]) * back[row]) * live[row])
    out[...] = jnp.swapaxes(jnp.stack(done), 0, 1)


def body(
    currents, counts, near_list, m2l_list, m2l_type, interp, compress, m2m, m2l, near_tiles, jacobi
):
    combos, leaves, unknowns = currents.shape
    rank = compress.shape[2]
    entries = m2l_list.shape[1]
    n = lax.axis_size("leaf")
    chans = lax.axis_size("chan")
    shape = jax.ShapeDtypeStruct

    def channel():
        return lax.div(lax.axis_index("chan") * combos, INC)

    def bound(kernel):
        return lambda *refs: kernel(channel, *refs)

    def permute(value, shift, cross):
        moves = []
        for leaf in range(n):
            for chan in range(chans):
                to = (leaf + shift) % n * chans + (chan ^ 1 if cross else chan)
                moves.append((leaf * chans + chan, to))
        return lax.ppermute(value, ("leaf", "chan"), moves)

    interp_t = jnp.swapaxes(interp, 1, 2)
    comp_t = jnp.swapaxes(compress, 1, 2)
    part = shape((leaves, combos, unknowns), F32)
    nodes = interp_t.shape[1]
    mine, live, comp_v, m2m_v, places, slots, kinds = call(
        bound(load_kernel),
        (
            part,
            shape((leaves, unknowns), F32),
            shape((rank, nodes), BF16),
            shape((leaves, rank, rank), BF16),
            shape(near_list.shape, jnp.int32),
            shape(m2l_list.shape, jnp.int32),
            shape(m2l_type.shape, jnp.int32),
        ),
        [HBM] * 7,
        [
            pltpu.SMEM((leaves,), jnp.int32),
            pltpu.VMEM(currents.shape, BF16),
            pltpu.VMEM(near_list.shape, jnp.int32),
            pltpu.VMEM(m2l_list.shape, jnp.int32),
            pltpu.SemaphoreType.DMA((7,)),
        ],
    )(*in_hbm(counts, currents, comp_t, m2m, near_list, m2l_list, m2l_type))
    packed, box = call(
        box_kernel,
        (shape((leaves + 1, combos, unknowns), BF16), shape((1, combos, 2 * rank), BF16)),
        [VMEM] * 4,
        cost=KCOST,
    )(mine, interp_t, comp_v, m2m_v)
    other = permute(box, 0, True)
    low = permute(packed, 1, False)

    high = permute(packed, -1, False)
    further = [permute(other, shift, True) for shift in range(2, n - 1)]
    after, _ = lax.optimization_barrier((packed, other))
    turned, first, apply, back, sources = call(
        bound(prepare_kernel),
        (
            shape((leaves, AHEAD, unknowns, unknowns), BF16),
            part,
            shape((leaves, 2 * rank, unknowns), BF16),
            shape((leaves, unknowns), F32),
            shape((n, 2 * rank, rank), BF16),
        ),
        [VMEM] * 8 + [HBM],
        [
            pltpu.VMEM((leaves, 2 * rank, unknowns), BF16),
            pltpu.VMEM((entries, rank, rank), BF16),
            pltpu.VMEM((n, rank, rank), F32),
            pltpu.SemaphoreType.DMA((entries,)),
        ],
        PCOST,
    )(after, near_tiles, interp_t, comp_v, m2m_v, slots, kinds, jacobi, *in_hbm(m2l))
    near = call(
        near_kernel, part, [VMEM] * 8, [pltpu.VMEM((3 * leaves, combos, unknowns), F32)], NCOST
    )(places, packed, low, high, near_tiles, turned, first, jacobi)
    return call(final_kernel, shape(currents.shape, F32), [VMEM] * (8 + len(further)))(
        sources, near, live, back, apply, box, low, high, *further
    )


def solution(mesh):
    placed = (
        P(("groups", "chan"), "leaf", None),
        P(("groups", "leaf")),
        P(("groups", "leaf"), None),
        P(("groups", "leaf"), None),
        P(("groups", "leaf"), None),
        P(("groups", "leaf"), None, None),
        P(),
        P(),
        P(),
        P(("groups", "leaf"), None, None, None),
        P(("groups", "leaf"), None, None),
    )
    return jax.shard_map(
        body,
        mesh=mesh,
        in_specs=placed,
        out_specs=P(("groups", "chan"), "leaf", None),
        check_vma=False,
    )
```

```python
import jax
import jax.numpy as jnp
from jax import lax
from jax.experimental import pallas as pl
from jax.experimental.pallas import tpu as pltpu
from jax.sharding import PartitionSpec as P

F32 = jnp.float32
BF16 = jnp.bfloat16
NT = (((1,), (1,)), ((), ()))
VMEM = pl.BlockSpec(memory_space=pltpu.VMEM)
HBM = pl.BlockSpec(memory_space=pltpu.HBM)
INC = 8
COST = 2 * 10**9
AHEAD = 3
KCOST = 2000000000
PCOST = 2000000000
NCOST = 1000000


def call(kernel, out_shape, in_specs, scratch=(), cost=COST):
    return pl.pallas_call(
        kernel,
        out_shape=out_shape,
        in_specs=in_specs,
        out_specs=jax.tree.map(lambda _: VMEM, out_shape),
        scratch_shapes=list(scratch),
        compiler_params=pltpu.CompilerParams(vmem_limit_bytes=16 << 20),
        cost_estimate=pl.CostEstimate(flops=cost, bytes_accessed=0, transcendentals=0),
    )


def in_hbm(*arrays):
    return [pltpu.with_memory_space_constraint(array, pltpu.HBM) for array in arrays]


def nt(a, b):
    return lax.dot_general(a, b, NT, preferred_element_type=F32)


def nn(a, b):
    return jnp.dot(a, b, preferred_element_type=F32)


def tn(a, b):
    return lax.dot_general(a, b, (((0,), (0,)), ((), ())), preferred_element_type=F32)


def halves(value):
    high = value.astype(BF16)
    return jnp.concatenate([high, (value - high.astype(F32)).astype(BF16)], axis=0)


def halves_sum(value):
    half = value.shape[0] // 2
    return value[:half] + value[half:]


def twice(value):
    return jnp.concatenate([value, value], axis=1)


def load_kernel(
    channel, counts, own, comp_t, m2m, near_list, m2l_list, m2l_type,
    mine, live, comp_out, m2m_out, places, slots, kinds, counts_s, own_s, near_s, list_s, sems,
):
    chan = channel()
    me = lax.axis_index("leaf")
    count = lax.axis_size("leaf")
    pairs = (
        (counts, counts_s),
        (own, own_s),
        (comp_t.at[chan], comp_out),
        (m2m.at[chan], m2m_out),
        (near_list, near_s),
        (m2l_list, list_s),
        (m2l_type, kinds),
    )
    copies = [pltpu.make_async_copy(a, b, sems.at[k]) for k, (a, b) in enumerate(pairs)]
    for copy in copies:
        copy.start()
    leaves, unknowns = live.shape
    lanes = lax.broadcasted_iota(jnp.int32, (1, unknowns), 1)
    copies[0].wait()
    for leaf in range(leaves):
        live[leaf : leaf + 1] = jnp.where(lanes < counts_s[leaf], 1.0, 0.0)
    copies[1].wait()
    mine[...] = jnp.swapaxes(own_s[...].astype(F32), 0, 1) * live[...][:, None, :]
    for copy in copies[2:]:
        copy.wait()
    places[...] = near_s[...] - (me - 1) * leaves
    slots[...] = lax.rem(me - list_s[...] + count, count)


def box_kernel(mine, interp_t, comp_t, m2m, packed, box):
    leaves, combos, unknowns = mine.shape
    x = mine[...].astype(BF16)
    packed[0:leaves] = x
    nodes = jnp.concatenate(
        [nt(x[leaf], interp_t[leaf]).astype(BF16) for leaf in range(leaves)], axis=0
    )
    moments = nt(nodes, comp_t[...]).astype(BF16)
    total = None
    for leaf in range(leaves):
        part = nn(moments[leaf * combos : (leaf + 1) * combos], m2m[leaf])
        total = part if total is None else total + part
    pair = twice(total).astype(BF16)
    packed[leaves] = jnp.concatenate(
        [pair, jnp.zeros((combos, unknowns - pair.shape[1]), BF16)], axis=1
    )
    box[0] = pair


def prepare_kernel(
    channel, packed, tiles, interp_t, comp_t, m2m, slots, kinds, jacobi, table,
    turned, first, apply, back, sources, expand, mats, sums, mat_sems,
):
    leaves = first.shape[0]
    chan = channel()
    kind = kinds[...]
    copies = [
        pltpu.make_async_copy(table.at[chan, kind[0, k]], mats.at[k], mat_sems.at[k])
        for k in range(mats.shape[0])
    ]
    for copy in copies:
        copy.start()
    comp = comp_t[...]
    tops = [jnp.max(jnp.abs(jacobi[leaf]), axis=0, keepdims=True).astype(F32) for leaf in range(leaves)]
    top = jnp.max(jnp.concatenate(tops, axis=0), axis=1, keepdims=True)
    scale = jnp.where(top > 2.0**90, 2.0**-30, jnp.where(top < 2.0**-90, 2.0**30, 1.0))
    back[...] = jnp.broadcast_to(1.0 / scale, back.shape)
    for leaf in range(leaves):
        expand[leaf] = halves(nn(comp, interp_t[leaf]) * scale[leaf : leaf + 1])
    for leaf in range(leaves):
        first[leaf] = nt(packed[leaf], tiles[leaf, 0])
        for k in range(turned.shape[1]):
            turned[leaf, k] = tiles[leaf, k + 1].T
    applied = [halves(halves_sum(nt(expand[leaf], jacobi[leaf]))) for leaf in range(leaves)]
    for leaf in range(leaves):
        child = m2m[leaf]
        apply[leaf] = halves(tn(jnp.concatenate([child, child], axis=0), applied[leaf]))
    for copy in copies:
        copy.wait()
    slot = slots[...]
    sums[...] = jnp.zeros_like(sums)
    for k in range(mats.shape[0]):
        sums[slot[0, k]] += mats[k].astype(F32)
    for place in range(sources.shape[0]):
        sources[place] = halves(sums[place])


def near_kernel(places, packed, low, high, tiles, turned, first, jacobi, near, beside):
    leaves, neighbours = places.shape
    ahead = turned.shape[1]
    places = places[...]
    beside[0:leaves] = low[0:leaves].astype(F32)
    beside[leaves : 2 * leaves] = packed[0:leaves].astype(F32)
    beside[2 * leaves : 3 * leaves] = high[0:leaves].astype(F32)
    sums = []
    for leaf in range(leaves):
        total = first[leaf]
        for k in range(1, neighbours):
            x = beside[places[leaf, k]].astype(BF16)
            if k <= ahead:
                total = total + nn(x, turned[leaf, k - 1])
            else:
                total = total + nt(tiles[leaf, k], x).T
        sums.append(halves(total))
    for leaf in range(leaves):
        near[leaf] = halves_sum(nt(sums[leaf], jacobi[leaf]))


def final_kernel(sources, near, live, back, apply, box, low, high, *refs):
    *further, out = refs
    leaves, lanes = near.shape[0], box.shape[2]
    boxes = [box[0], low[leaves, :, :lanes]] + [ref[0] for ref in further] + [high[leaves, :, :lanes]]
    local = nn(jnp.concatenate(boxes, axis=1), sources[...].reshape(-1, sources.shape[2]))
    local = twice(local).astype(BF16)
    done = []
    for leaf in range(leaves):
        row = slice(leaf, leaf + 1)
        done.append((near[leaf] + nn(local, apply[leaf]) * back[row]) * live[row])
    out[...] = jnp.swapaxes(jnp.stack(done), 0, 1)


def body(
    currents, counts, near_list, m2l_list, m2l_type, interp, compress, m2m, m2l, near_tiles, jacobi
):
    combos, leaves, unknowns = currents.shape
    rank = compress.shape[2]
    entries = m2l_list.shape[1]
    n = lax.axis_size("leaf")
    chans = lax.axis_size("chan")
    shape = jax.ShapeDtypeStruct

    def channel():
        return lax.div(lax.axis_index("chan") * combos, INC)

    def bound(kernel):
        return lambda *refs: kernel(channel, *refs)

    def permute(value, shift, cross):
        moves = []
        for leaf in range(n):
            for chan in range(chans):
                to = (leaf + shift) % n * chans + (chan ^ 1 if cross else chan)
                moves.append((leaf * chans + chan, to))
        return lax.ppermute(value, ("leaf", "chan"), moves)

    interp_t = jnp.swapaxes(interp, 1, 2)
    comp_t = jnp.swapaxes(compress, 1, 2)
    part = shape((leaves, combos, unknowns), F32)
    nodes = interp_t.shape[1]
    mine, live, comp_v, m2m_v, places, slots, kinds = call(
        bound(load_kernel),
        (
            part,
            shape((leaves, unknowns), F32),
            shape((rank, nodes), BF16),
            shape((leaves, rank, rank), BF16),
            shape(near_list.shape, jnp.int32),
            shape(m2l_list.shape, jnp.int32),
            shape(m2l_type.shape, jnp.int32),
        ),
        [HBM] * 7,
        [
            pltpu.SMEM((leaves,), jnp.int32),
            pltpu.VMEM(currents.shape, BF16),
            pltpu.VMEM(near_list.shape, jnp.int32),
            pltpu.VMEM(m2l_list.shape, jnp.int32),
            pltpu.SemaphoreType.DMA((7,)),
        ],
    )(*in_hbm(counts, currents, comp_t, m2m, near_list, m2l_list, m2l_type))
    packed, box = call(
        box_kernel,
        (shape((leaves + 1, combos, unknowns), BF16), shape((1, combos, 2 * rank), BF16)),
        [VMEM] * 4,
        cost=KCOST,
    )(mine, interp_t, comp_v, m2m_v)
    other = permute(box, 0, True)
    low = permute(packed, 1, False)

    high = permute(packed, -1, False)
    further = [permute(other, shift, True) for shift in range(2, n - 1)]
    after, _ = lax.optimization_barrier((packed, other))
    turned, first, apply, back, sources = call(
        bound(prepare_kernel),
        (
            shape((leaves, AHEAD, unknowns, unknowns), BF16),
            part,
            shape((leaves, 2 * rank, unknowns), BF16),
            shape((leaves, unknowns), F32),
            shape((n, 2 * rank, rank), BF16),
        ),
        [VMEM] * 8 + [HBM],
        [
            pltpu.VMEM((leaves, 2 * rank, unknowns), BF16),
            pltpu.VMEM((entries, rank, rank), BF16),
            pltpu.VMEM((n, rank, rank), F32),
            pltpu.SemaphoreType.DMA((entries,)),
        ],
        PCOST,
    )(after, near_tiles, interp_t, comp_v, m2m_v, slots, kinds, jacobi, *in_hbm(m2l))
    near = call(
        near_kernel, part, [VMEM] * 8, [pltpu.VMEM((3 * leaves, combos, unknowns), F32)], NCOST
    )(places, packed, low, high, near_tiles, turned, first, jacobi)
    return call(final_kernel, shape(currents.shape, F32), [VMEM] * (8 + len(further)))(
        sources, near, live, back, apply, box, low, high, *further
    )


def solution(mesh):
    placed = (
        P(("groups", "chan"), "leaf", None),
        P(("groups", "leaf")),
        P(("groups", "leaf"), None),
        P(("groups", "leaf"), None),
        P(("groups", "leaf"), None),
        P(("groups", "leaf"), None, None),
        P(),
        P(),
        P(),
        P(("groups", "leaf"), None, None, None),
        P(("groups", "leaf"), None, None),
    )
    return jax.shard_map(
        body,
        mesh=mesh,
        in_specs=placed,
        out_specs=P(("groups", "chan"), "leaf", None),
        check_vma=False,
    )
```
